128 devices in a mesh: lat: 8 (over y, z_hi), lon: 16 (over z_lo, x, core).
Axes of the slice: x: 4, y: 4, z: 4 (z_hi: 2, z_lo: 2; z = z_hi * 2 + z_lo), core: 2. Of those that a mesh axis runs over, the one named last changes fastest.
Arguments:
- tokens: bfloat16 [1, 96, 384, 384], P(None, 'lat', 'lon'), may hold values from -6 to 6
- cotangent: bfloat16 [1, 48, 192, 768], P(None, 'lat', 'lon'), may hold values from -6 to 6
- bias_one: float32 [17, 6, 3312], replicated, may hold values from -4 to 324
- qkv_one: bfloat16 [192, 576], replicated, may hold values from -0.4375 to 0.4375
- proj_one: bfloat16 [192, 192], replicated, may hold values from -0.4375 to 0.4375
- up_one: bfloat16 [192, 768], replicated, may hold values from -0.4375 to 0.4375
- down_one: bfloat16 [768, 192], replicated, may hold values from -0.21875 to 0.21875
- merge_weight: bfloat16 [768, 384], replicated, may hold values from -0.21875 to 0.21875
- bias_two: float32 [9, 12, 3312], replicated, may hold values from -4 to 324
- qkv_two: bfloat16 [384, 1152], replicated, may hold values from -0.3125 to 0.3125
- proj_two: bfloat16 [384, 384], replicated, may hold values from -0.3125 to 0.3125
- up_two: bfloat16 [384, 1536], replicated, may hold values from -0.3125 to 0.3125
- down_two: bfloat16 [1536, 384], replicated, may hold values from -0.15625 to 0.15625
Outputs:
- level_two_out: float32 [1, 48, 192, 768], P(None, 'lat', 'lon')
- token_grad: float32 [1, 96, 384, 384], P(None, 'lat', 'lon')
- qkv_one_grad: float32 [192, 576], replicated
- proj_one_grad: float32 [192, 192], replicated
- up_one_grad: float32 [192, 768], replicated
- down_one_grad: float32 [768, 192], replicated
- merge_grad: float32 [768, 384], replicated
- qkv_two_grad: float32 [384, 1152], replicated
- proj_two_grad: float32 [384, 384], replicated
- up_two_grad: float32 [384, 1536], replicated
- down_two_grad: float32 [1536, 384], replicated
The draws below stay inside these ranges and needn't reach their ends.
All inputs are finite; a program needn't handle non-finite values.
Results may differ from the reference program's by a relative error of at most 0.025.
Values may be sent and summed in bfloat16 or wider, within the bound.
No kernel may reach another device: no remote copies, remote signals or barrier semaphores. Data moves between devices by JAX's collectives and lax.ppermute only.
A program may use at most 256 MiB of HBM per device.

```python
import jax
import jax.numpy as jnp
from jax import lax

C1 = 192
C2 = 384
HEAD = 32
LEVELS = 2
WLAT = 6
WLON = 12
BATCH = 1
WINDOW = 144
H1 = 6
H2 = 12
NLAT1 = 96
NLON1 = 384
NLAT2 = 48
NLON2 = 192
TYPES1 = 17
TYPES2 = 9
BIAS_LEN = 3312
TOKENS2 = 18432


def base_table(key, type_count, head_count, entry_count):
    return jax.random.truncated_normal(key, -4.0, 4.0, (type_count, head_count, entry_count), jnp.float32)


def draw_bias_one(key, part):
    key = jax.random.fold_in(key, 11)
    table = base_table(key, TYPES1, H1, BIAS_LEN)
    return table


def draw_bias_two(key, part):
    key = jax.random.fold_in(key, 13)
    table = base_table(key, TYPES2, H2, BIAS_LEN)
    return table


def level_of(key, extent, cuts, smallest, high):
    def one(dim, shards_of):
        steps = jax.random.uniform(jax.random.fold_in(jax.random.fold_in(key, 6), dim), (shards_of,), jnp.float32, smallest / len(cuts), high / len(cuts))
        return jnp.repeat(jnp.exp(steps), extent[dim] // shards_of).reshape((-1,) + (1,) * (len(extent) - dim - 1))

    factor_of = one(*cuts[0])
    for cut in cuts[1:]:
        factor_of = factor_of * one(*cut)
    return factor_of


def bell_draw(rng, shape, scale, bound, shards=(), held_as=jnp.bfloat16):
    values = jax.random.normal(rng, shape, jnp.float32) * scale
    if len(shards) > 0:
        values = level_of(rng, shape, shards, -0.22, 0.18) * values
    return jnp.clip(values, min=-bound, max=bound).astype(held_as)


def setup_inputs(seed: int = 0) -> dict:
    keys = jax.random.split(jax.random.key(seed), 14)
    return {
        "tokens": bell_draw(keys[0], (BATCH, NLAT1, NLON1, LEVELS * C1), 1.0, 6.0, ((1, 8), (2, 16))),
        "cotangent": bell_draw(keys[1], (BATCH, NLAT2, NLON2, LEVELS * C2), 1.0, 6.0, ((1, 8), (2, 16))),
        "bias_one": draw_bias_one(jax.random.fold_in(keys[13], 71), 0),
        "qkv_one": bell_draw(keys[3], (C1, 3 * C1), C1 ** -0.5, 0.4375),
        "proj_one": bell_draw(keys[4], (C1, C1), C1 ** -0.5, 0.4375),
        "up_one": bell_draw(keys[5], (C1, 4 * C1), C1 ** -0.5, 0.4375),
        "down_one": bell_draw(keys[6], (4 * C1, C1), (4 * C1) ** -0.5, 0.21875),
        "merge_weight": bell_draw(keys[7], (4 * C1, C2), (4 * C1) ** -0.5, 0.21875),
        "bias_two": draw_bias_two(jax.random.fold_in(keys[13], 71), 0),
        "qkv_two": bell_draw(keys[9], (C2, 3 * C2), C2 ** -0.5, 0.3125),
        "proj_two": bell_draw(keys[10], (C2, C2), C2 ** -0.5, 0.3125),
        "up_two": bell_draw(keys[11], (C2, 4 * C2), C2 ** -0.5, 0.3125),
        "down_two": bell_draw(keys[12], (4 * C2, C2), (4 * C2) ** -0.5, 0.15625),
    }


EPSILON = 1e-05
MASKED = -1e+30
HIGHEST = lax.Precision.HIGHEST

def normalize(values):
    average = lax.optimization_barrier(jnp.mean(values, axis=-1, keepdims=True))
    centred = values - average
    spread = lax.optimization_barrier(jnp.mean(centred * centred, axis=-1, keepdims=True))
    return centred * lax.rsqrt(spread + EPSILON)

def widen(values):
    return lax.optimization_barrier(values).astype(jnp.float32)

def offset_matrix(bias_rows):
    leading = bias_rows.shape[:-1]
    split_rows = bias_rows.reshape(leading + (LEVELS, LEVELS, WLAT, WLAT, 2 * WLON - 1))
    relative = jnp.arange(2 * WLON - 1).reshape(2 * WLON - 1, 1, 1)
    first_col = jnp.arange(WLON).reshape(1, WLON, 1)
    second_col = jnp.arange(WLON).reshape(1, 1, WLON)
    selector = (first_col - second_col + WLON - 1 == relative).astype(bias_rows.dtype)
    spread_out = jnp.einsum('...xyabr,rpq->...xapybq', split_rows, selector, precision=HIGHEST)
    return spread_out.reshape(leading + (WINDOW, WINDOW))

def to_windows(grid):
    batch_size, row_count, col_count, level_count, feat_count = grid.shape
    lat_count = row_count // WLAT
    lon_count = col_count // WLON
    blocks = grid.reshape(batch_size, lat_count, WLAT, lon_count, WLON, level_count, feat_count)
    blocks = blocks.transpose(1, 0, 3, 5, 2, 4, 6)
    return blocks.reshape(lat_count, batch_size * lon_count, level_count * WLAT * WLON, feat_count)

def from_windows(blocks, batch_size, row_count, col_count):
    lat_count = blocks.shape[0]
    feat_count = blocks.shape[-1]
    lon_count = col_count // WLON
    grid = blocks.reshape(lat_count, batch_size, lon_count, LEVELS, WLAT, WLON, feat_count)
    grid = grid.transpose(1, 0, 4, 2, 5, 3, 6)
    return grid.reshape(batch_size, row_count, col_count, LEVELS, feat_count)

def split_heads(blocks, width):
    head_shape = blocks.shape[:-1] + (width // HEAD, HEAD)
    return (blocks[..., :width].reshape(head_shape), blocks[..., width:2 * width].reshape(head_shape), blocks[..., 2 * width:].reshape(head_shape))

def attend(queries, key_rows, value_rows, offsets, usable):
    factor = HEAD ** (-0.5)
    scores = jnp.einsum('aoqhd,aokhd->aohqk', widen(queries), widen(key_rows), precision=HIGHEST) * factor + offsets
    scores = jnp.where(usable, scores, MASKED)
    chances = jax.nn.softmax(scores, axis=-1)
    rounded = widen(chances.astype(jnp.bfloat16))
    weighted = jnp.einsum('aohqk,aokhd->aoqhd', rounded, widen(value_rows), precision=HIGHEST)
    return (weighted.astype(jnp.bfloat16), chances)

def attend_back(queries, key_rows, value_rows, chances, grad_weighted):
    factor = HEAD ** (-0.5)
    rounded = widen(chances.astype(jnp.bfloat16))
    grad_rounded = widen(grad_weighted.astype(jnp.bfloat16))
    grad_chances = jnp.einsum('aoqhd,aokhd->aohqk', grad_rounded, widen(value_rows), precision=HIGHEST)
    grad_values = jnp.einsum('aohqk,aoqhd->aokhd', rounded, grad_rounded, precision=HIGHEST)
    inner = lax.optimization_barrier(jnp.sum(grad_chances * chances, axis=-1, keepdims=True))
    grad_scores = widen((chances * (grad_chances - inner) * factor).astype(jnp.bfloat16))
    grad_queries = jnp.einsum('aohqk,aokhd->aoqhd', grad_scores, widen(key_rows), precision=HIGHEST)
    grad_keys = jnp.einsum('aohqk,aoqhd->aokhd', grad_scores, widen(queries), precision=HIGHEST)
    return (grad_queries, grad_keys, grad_values)

def shifted_windows(grid):
    moved = jnp.roll(grid, -(WLON // 2), axis=2)
    moved = jnp.pad(moved, ((0, 0), (WLAT // 2, WLAT // 2), (0, 0), (0, 0), (0, 0)))
    return to_windows(moved)

def unshift(blocks, batch_size, lat_total, lon_total):
    grid = from_windows(blocks, batch_size, lat_total + WLAT, lon_total)
    grid = grid[:, WLAT // 2:WLAT // 2 + lat_total]
    return jnp.roll(grid, WLON // 2, axis=2)

def key_mask(lat_total):
    lat_count = lat_total // WLAT + 1
    global_rows = jnp.arange(lat_total + WLAT) - WLAT // 2
    inside = ((global_rows >= 0) & (global_rows < lat_total)).reshape(lat_count, 1, WLAT, 1)
    return jnp.broadcast_to(inside, (lat_count, LEVELS, WLAT, WLON)).reshape(lat_count, WINDOW)

def band_attention(blocks, offsets, usable, width):

    def one_band(inputs):
        block, offset_rows, usable_row = inputs
        queries, key_rows, value_rows = split_heads(block[None], width)
        weighted, chances = attend(queries, key_rows, value_rows, offset_rows[None, None], usable_row[None, None, None, None])
        return weighted[0].reshape(block.shape[:2] + (width,))
    return lax.map(one_band, (blocks, offsets, usable))

def band_attention_back(blocks, offsets, usable, grad_blocks, width):

    def one_band(inputs):
        block, offset_rows, usable_row, grad_row = inputs
        queries, key_rows, value_rows = split_heads(block[None], width)
        weighted, chances = attend(queries, key_rows, value_rows, offset_rows[None, None], usable_row[None, None, None, None])
        grads = attend_back(queries, key_rows, value_rows, chances, grad_row[None].reshape(queries.shape))
        return jnp.concatenate([grad_part[0].reshape(block.shape[:2] + (width,)) for grad_part in grads], axis=-1)
    return lax.map(one_band, (blocks, offsets, usable, grad_blocks))

def level_forward(grid, weights, bias_table, width):
    qkv_weight, proj_weight, up_weight, down_weight = weights
    batch_size, lat_total, lon_total = grid.shape[:3]
    normed = normalize(grid).astype(jnp.bfloat16)
    projected = jnp.dot(normed.reshape(-1, width), qkv_weight, preferred_element_type=jnp.float32).astype(jnp.bfloat16)
    projected = lax.optimization_barrier(projected.reshape(grid.shape[:4] + (3 * width,)))
    blocks = shifted_windows(projected)
    offsets = offset_matrix(bias_table)
    usable = key_mask(lat_total)
    weighted = band_attention(blocks, offsets, usable, width)
    attended = unshift(weighted, batch_size, lat_total, lon_total)
    middle = grid + jnp.dot(attended.reshape(-1, width), proj_weight, preferred_element_type=jnp.float32).reshape(grid.shape)
    normed_two = normalize(middle).astype(jnp.bfloat16)
    raised = jnp.dot(normed_two.reshape(-1, width), up_weight, preferred_element_type=jnp.float32)
    activated = jax.nn.gelu(raised).astype(jnp.bfloat16)
    result = middle + jnp.dot(activated, down_weight, preferred_element_type=jnp.float32).reshape(grid.shape)
    return (result, (normed, blocks, offsets, usable, attended, middle, normed_two, raised, activated))

def level_backward(grid, saved, grad_result, weights, width):
    qkv_weight, proj_weight, up_weight, down_weight = weights
    normed, blocks, offsets, usable, attended, middle, normed_two, raised, activated = saved
    batch_size, lat_total, lon_total = grid.shape[:3]
    grad_flat = grad_result.reshape(-1, width).astype(jnp.bfloat16)
    grad_down = jnp.dot(activated.T, grad_flat, preferred_element_type=jnp.float32)
    grad_active = jnp.dot(grad_flat, down_weight.T, preferred_element_type=jnp.float32)
    grad_raised = jax.vjp(jax.nn.gelu, raised)[1](grad_active)[0].astype(jnp.bfloat16)
    grad_up = jnp.dot(normed_two.reshape(-1, width).T, grad_raised, preferred_element_type=jnp.float32)
    grad_normed_two = jnp.dot(grad_raised, up_weight.T, preferred_element_type=jnp.float32).reshape(grid.shape)
    grad_middle = grad_result + jax.vjp(normalize, middle)[1](grad_normed_two)[0]
    grad_middle_flat = grad_middle.reshape(-1, width).astype(jnp.bfloat16)
    grad_proj = jnp.dot(attended.reshape(-1, width).T, grad_middle_flat, preferred_element_type=jnp.float32)
    grad_attended = jnp.dot(grad_middle_flat, proj_weight.T, preferred_element_type=jnp.float32).reshape(grid.shape)
    grad_windows = shifted_windows(grad_attended)
    grad_blocks = band_attention_back(blocks, offsets, usable, grad_windows, width)
    grad_projected = unshift(grad_blocks, batch_size, lat_total, lon_total).reshape(-1, 3 * width).astype(jnp.bfloat16)
    grad_qkv = jnp.dot(normed.reshape(-1, width).T, grad_projected, preferred_element_type=jnp.float32)
    grad_normed = jnp.dot(grad_projected, qkv_weight.T, preferred_element_type=jnp.float32).reshape(grid.shape)
    grad_grid = grad_middle + jax.vjp(normalize, grid)[1](grad_normed)[0]
    return (grad_grid, (grad_qkv, grad_proj, grad_up, grad_down))

def merge_forward(grid, merge_weight):
    batch_size, lat_total, lon_total = grid.shape[:3]
    grouped = grid.reshape(batch_size, lat_total // 2, 2, lon_total // 2, 2, LEVELS, -1)
    grouped = grouped.transpose(0, 1, 3, 5, 2, 4, 6).reshape(batch_size, lat_total // 2, lon_total // 2, LEVELS, -1)
    merged_norm = normalize(grouped).astype(jnp.bfloat16)
    merged = jnp.dot(merged_norm.reshape(-1, merge_weight.shape[0]), merge_weight, preferred_element_type=jnp.float32)
    return (merged.reshape(grouped.shape[:4] + (merge_weight.shape[1],)), grouped, merged_norm)

def merge_backward(grouped, merged_norm, grad_merged, merge_weight):
    grad_flat = grad_merged.reshape(-1, merge_weight.shape[1]).astype(jnp.bfloat16)
    grad_weight = jnp.dot(merged_norm.reshape(-1, merge_weight.shape[0]).T, grad_flat, preferred_element_type=jnp.float32)
    grad_norm = jnp.dot(grad_flat, merge_weight.T, preferred_element_type=jnp.float32).reshape(grouped.shape)
    grad_grouped = jax.vjp(normalize, grouped)[1](grad_norm)[0]
    batch_size, half_lat, half_lon = grouped.shape[:3]
    regrid = grad_grouped.reshape(batch_size, half_lat, half_lon, LEVELS, 2, 2, -1)
    regrid = regrid.transpose(0, 1, 4, 2, 5, 3, 6)
    return (regrid.reshape(batch_size, 2 * half_lat, 2 * half_lon, LEVELS, -1), grad_weight)

def reference(tokens, cotangent, bias_one, qkv_one, proj_one, up_one, down_one, merge_weight, bias_two, qkv_two, proj_two, up_two, down_two):
    weights_one = (qkv_one, proj_one, up_one, down_one)
    weights_two = (qkv_two, proj_two, up_two, down_two)
    grid_one = tokens.astype(jnp.float32).reshape(BATCH, NLAT1, NLON1, LEVELS, C1)
    out_one, saved_one = level_forward(grid_one, weights_one, bias_one, C1)
    grid_two, grouped, merged_norm = merge_forward(out_one, merge_weight)
    out_two, saved_two = level_forward(grid_two, weights_two, bias_two, C2)
    grad_two = cotangent.astype(jnp.float32).reshape(out_two.shape)
    grad_grid_two, grads_two = level_backward(grid_two, saved_two, grad_two, weights_two, C2)
    grad_out_one, grad_merge = merge_backward(grouped, merged_norm, grad_grid_two, merge_weight)
    grad_grid_one, grads_one = level_backward(grid_one, saved_one, grad_out_one, weights_one, C1)
    factor = TOKENS2 ** (-0.5)
    return (out_two.reshape(BATCH, NLAT2, NLON2, LEVELS * C2), grad_grid_one.reshape(BATCH, NLAT1, NLON1, LEVELS * C1), grads_one[0] * factor, grads_one[1] * factor, grads_one[2] * factor, grads_one[3] * factor, grad_merge * factor, grads_two[0] * factor, grads_two[1] * factor, grads_two[2] * factor, grads_two[3] * factor)
```

```python
import functools

import jax
import jax.numpy as jnp
import numpy as np
from jax import lax
from jax.experimental import pallas as pl
from jax.experimental.pallas import tpu as pltpu
from jax.sharding import Mesh, PartitionSpec as P

C1 = 192
C2 = 384
HEAD = 32
LEVELS = 2
WLAT = 6
WLON = 12
WINDOW = 144
REL = 2 * WLON - 1
COLUMN = LEVELS * WLAT
FACTOR = HEAD**-0.5
EPSILON = 1e-05
MASKED = -1e30
GROUPS_ONE = ((0, 4), (4, 2))
GROUPS_TWO = ((0, 4), (4, 4), (8, 4))
STRIPS = (112, 112, 48)
VMEM_BYTES = 60 * 1024 * 1024
LANES = 128
CHIPS = 64
UPPER_BLOCK = 128
LOWER_BLOCK = 32
F32 = jnp.float32
BF16 = jnp.bfloat16


def constants():
    select = np.zeros((2, 432, 288), np.float32)
    for col in range(36):
        half, source = (0, 6 + col) if col < 18 else (1, col - 18)
        for level in range(2):
            for a in range(6):
                select[level, col * 12 + level * 6 + a, half * 144 + a * 24 + source] = 1
    own = {}
    gather = np.zeros((3, 576, 432), np.float32)
    for pr in range(2):
        for pc in range(2):
            for out_col in range(12):
                for level in range(2):
                    for out_row in range(6):
                        row, col = 3 + 2 * out_row + pr, 6 + 2 * out_col + pc
                        place = (pr * 2 + pc) * 144 + out_col * 12 + level * 6 + out_row
                        gather[row // 6, place, col * 12 + level * 6 + row % 6] = 1
                        own[row, col, level] = place
    cot_select = np.zeros((144, 288), np.float32)
    for out_col in range(12):
        for out_row in range(6):
            for level in range(2):
                up, right = out_row < 3, out_col >= 6
                block = (2 if up else 0) + (1 if right else 0)
                col = out_col - 6 if right else 6 + out_col
                place = out_col * 12 + level * 6 + out_row
                cot_select[place, block * 72 + out_row % 3 * 24 + level * 12 + col] = 1
    strips = np.zeros((sum(STRIPS), 576), np.float32)
    back_own = np.zeros((576, 576), np.float32)
    back_strips = np.zeros((576, sum(STRIPS)), np.float32)
    for row in range(6, 18):
        for col in range(24):
            for level in range(2):
                target = (row - 6) // 6 * 288 + col * 12 + level * 6 + row % 6
                if row <= 14 and col >= 6:
                    back_own[target, own[row, col, level]] = 1
                    continue
                if row <= 14:
                    place = (row - 6) * 12 + col * 2 + level
                    sent = (row, 24 + col, level)
                elif col >= 6:
                    place = STRIPS[0] + (row - 15) * 36 + (col - 6) * 2 + level
                    sent = (row - 12, col, level)
                else:
                    place = STRIPS[0] + STRIPS[1] + (row - 15) * 12 + col * 2 + level
                    sent = (row - 12, 24 + col, level)
                back_strips[target, place] = 1
                strips[place, own[sent]] = 1
    return tuple(jnp.asarray(v, BF16) for v in (select, gather, cot_select, strips, back_own, back_strips))


def bias_constants():
    z1, z2, a1, a2, r = (v.reshape(-1) for v in np.indices((LEVELS, LEVELS, WLAT, WLAT, REL)))
    half = WLAT // 2
    kind = np.where((a1 < half) & (a2 < half), 0.0, np.where((a1 >= half) & (a2 >= half), 1.0, 2.0))
    rows = (z2 * WLAT + a2)[None] == np.arange(16)[:, None]
    lanes = (r * COLUMN + z1 * WLAT + a1)[:, None] == np.arange(REL * COLUMN)[None]
    return (
        jnp.asarray(kind[None], F32),
        jnp.asarray(rows, F32),
        jnp.asarray(lanes.astype(np.float32), BF16),
    )


def blocks_of_heads():
    mask = (np.arange(576)[:, None] // WINDOW == np.arange(128)[None] // HEAD).astype(np.float32)
    fold = (np.arange(WINDOW)[:, None] == np.arange(576)[None] % WINDOW).astype(np.float32)
    return tuple(jnp.asarray(v, BF16) for v in (mask, mask.T, fold))


def nn(left, right):
    return jnp.dot(left, right, preferred_element_type=F32)


def nt(left, right):
    return lax.dot_general(left, right, (((1,), (1,)), ((), ())), preferred_element_type=F32)


def tn(left, right):
    return lax.dot_general(left, right, (((0,), (0,)), ((), ())), preferred_element_type=F32)


def layer_norm(values):
    average = jnp.mean(values, axis=-1, keepdims=True)
    centred = values - average
    scale = lax.rsqrt(jnp.mean(centred * centred, axis=-1, keepdims=True) + EPSILON)
    return centred * scale, scale


def layer_norm_back(grad, normed, scale):
    first = jnp.mean(grad, axis=-1, keepdims=True)
    second = jnp.mean(grad * normed, axis=-1, keepdims=True)
    return scale * (grad - first - normed * second)


GELU_A = (2.0 / np.pi) ** 0.5
GELU_B = 0.044715


def gelu(values):
    tanh = jnp.tanh(GELU_A * (values + GELU_B * (values * values * values)))
    return 0.5 * values * (1.0 + tanh)


def gelu_both(values):
    square = values * values
    tanh = jnp.tanh(GELU_A * values * (1.0 + GELU_B * square))
    half = 0.5 * (1.0 + tanh)
    slope = half + 0.5 * values * (1.0 - tanh * tanh) * (GELU_A * (1.0 + 3.0 * GELU_B * square))
    return values * half, slope


def spread(values, mask, heads):
    return jnp.concatenate([values] * heads, axis=0) * mask[: heads * WINDOW, : heads * HEAD]


def pull(left, right, mask_t, fold, heads):
    both = tn(left, right).astype(BF16) * mask_t[: heads * HEAD, : heads * WINDOW]
    return nt(fold[:, : heads * WINDOW], both)


def attend(queries, keys, values, bias, mask, mask_t, fold, heads):
    scores = nt(keys, spread(queries, mask, heads)) * FACTOR + bias
    powers = jnp.exp(scores - jnp.max(scores, axis=0, keepdims=True))
    chances = powers * (1.0 / jnp.sum(powers, axis=0, keepdims=True))
    return pull(values, chances.astype(BF16), mask_t, fold, heads), chances


def attend_back(queries, keys, values, chances, grad, mask, mask_t, fold, heads):
    grads = spread(grad, mask, heads)
    grad_chances = nt(values, grads)
    grad_values = nn(chances.astype(BF16), grads)
    inner = jnp.sum(grad_chances * chances, axis=0, keepdims=True)
    grad_scores = (chances * (grad_chances - inner) * FACTOR).astype(BF16)
    grad_keys = nn(grad_scores, spread(queries, mask, heads))
    grad_queries = pull(keys, grad_scores, mask_t, fold, heads)
    return grad_queries, grad_keys, grad_values


def bias_kernel(ids, one, two, kind, rows, lanes, first_ref, second_ref, two_out_ref, pieces, table):
    band = ids[0]

    def window(source, index):
        count = source.shape[0] - 1
        value = source[lax.rem(index + count, count)]
        mixed = jnp.where(
            kind[...] == 0.0, source[count], jnp.where(kind[...] == 1.0, source[0], MASKED)
        )
        return jnp.where(lax.rem(index + count, count) == 0, mixed, value)

    slot = 0
    for source, index in ((one, 2 * band - 1), (one, 2 * band), (one, 2 * band + 1), (two, band)):
        rest = window(source, index)
        for piece in range(3):
            taken = rest.astype(BF16).astype(F32)
            rest = rest - taken
            for h in range(taken.shape[0]):
                low = (slot + h) * 16
                value = jnp.where(rows[...] > 0.0, taken[h : h + 1, :], 0.0)
                pieces[piece, low : low + 16, :] = value.astype(BF16)
        slot += source.shape[1]
    table[...] = nn(pieces[0], lanes[...]) + nn(pieces[1], lanes[...]) + nn(pieces[2], lanes[...])

    for base, count, groups, targets in (
        (0, 3, GROUPS_ONE, (first_ref, second_ref)),
        (18, 1, GROUPS_TWO, (two_out_ref, two_out_ref, two_out_ref)),
    ):
        for row in range(count):
            for index, (start, heads) in enumerate(groups):
                target = targets[index]
                place = row if count == 3 else index
                low = [(base + row * 6 + start + h) * 16 for h in range(heads)]
                for o2 in range(WLON):
                    left = (WLON - 1 - o2) * COLUMN
                    piece = [table[at : at + COLUMN, left : left + WINDOW] for at in low]
                    target[place, o2 * COLUMN : (o2 + 1) * COLUMN, :] = jnp.concatenate(piece, axis=1)


def expand_bias(*operands):
    return pl.pallas_call(
        bias_kernel,
        in_specs=specs(len(operands)),
        out_shape=(
            jax.ShapeDtypeStruct((3, WINDOW, 576), F32),
            jax.ShapeDtypeStruct((3, WINDOW, 288), F32),
            jax.ShapeDtypeStruct((3, WINDOW, 576), F32),
        ),
        scratch_shapes=[
            pltpu.VMEM((3, 480, operands[1].shape[2]), BF16),
            pltpu.VMEM((480, REL * COLUMN), F32),
        ],
        compiler_params=pltpu.CompilerParams(vmem_limit_bytes=VMEM_BYTES),
        name="bias_expand",
    )(*operands)


def pack_kernel(tokens, cot, right_ref, up_ref):
    for out, row, cot_row in ((right_ref, 0, 0), (up_ref, 3, 3)):
        out[:9] = tokens[row : row + 9]
        for r in range(3):
            value = cot[cot_row + r].astype(F32)
            out[9 + r] = jnp.concatenate([value[:, :C2], value[:, C2:]], axis=0).astype(BF16)


def pack(tokens, cot):
    shape = jax.ShapeDtypeStruct((12, 24, 2 * C1), BF16)
    return pl.pallas_call(pack_kernel, out_shape=(shape, shape), name="pack")(tokens, cot)


def put(packed, base, value):
    half, count = packed.shape[1], value.shape[0]
    for j in range(value.shape[1] // LANES):
        start, stop = base + j * count, base + (j + 1) * count
        lanes = value[:, j * LANES : (j + 1) * LANES]
        for part in range(2):
            low, high = max(start, part * half), min(stop, (part + 1) * half)
            if low < high:
                packed[part, low - part * half : high - part * half, :] = lanes[low - start : high - start]
    return base + value.shape[0] * value.shape[1] // LANES


def take(packed, base, count, columns):
    half, lanes = packed.shape[1], []
    for j in range(columns):
        start, stop, rows = base + j * count, base + (j + 1) * count, []
        for part in range(2):
            low, high = max(start, part * half), min(stop, (part + 1) * half)
            if low < high:
                rows.append(packed[part, low - part * half : high - part * half, :])
        lanes.append(rows[0] if len(rows) == 1 else jnp.concatenate(rows, axis=0))
    return jnp.concatenate(lanes, axis=1).astype(F32)


def send_halves(ids, packed, mine_ref, theirs_ref, sems):
    copies = [
        pltpu.make_async_copy(packed.at[ids[2]], mine_ref, sems.at[0]),
        pltpu.make_async_copy(packed.at[1 - ids[2]], theirs_ref, sems.at[1]),
    ]
    for copy in copies:
        copy.start()
    for copy in copies:
        copy.wait()


def upper_kernel(
    ids, own, cot_own, right, up, diag,
    bias_a, bias_b, bias_two,
    qkv_one, proj_one, up_one, down_one, merge, qkv_two, proj_two, up_two, down_two,
    select, gather, cot_select, strips, mask_ref, mask_t_ref, fold_ref,
    out_ref, xw_ref, grad_ref, lon_ref, lat_ref, corner_ref, mine_ref, theirs_ref,
    q_ref, k_ref, v_ref, att_ref, xm_ref, am_ref, one_ref, p_ref, packed, sems,
):
    mask, mask_t, fold = mask_ref[...], mask_t_ref[...], fold_ref[...]

    def rows_of(block, start, count):
        return [block[start + r].astype(F32) for r in range(count)]

    for wr in range(3):
        if wr == 0:
            left, other = rows_of(up, 0, 6), rows_of(diag, 0, 6)
        elif wr == 1:
            left = rows_of(up, 6, 3) + rows_of(own, 0, 3)
            other = rows_of(diag, 6, 3) + rows_of(right, 0, 3)
        else:
            left, other = rows_of(own, 3, 6), rows_of(right, 3, 6)
        source = jnp.concatenate(left + other, axis=0).astype(BF16)
        cells = nn(select[0], source[:, :C1]) + nn(select[1], source[:, C1:])
        xw_ref[wr] = cells.astype(BF16)
        normed = layer_norm(cells)[0].astype(BF16)
        projected = nn(normed, qkv_one[...]).astype(BF16)
        q_ref[wr] = projected[:, :C1]
        k_ref[wr] = projected[:, C1 : 2 * C1]
        v_ref[wr] = projected[:, 2 * C1 :]

    @pl.loop(0, 3)
    def _(wr):
        for wc in range(3):
            rows = slice(wc * WINDOW, (wc + 1) * WINDOW)
            for start, heads in GROUPS_ONE:
                lanes = slice(start * HEAD, (start + heads) * HEAD)
                bias = bias_a[wr] if heads == 4 else bias_b[wr]
                att_ref[wr, rows, lanes] = attend(
                    q_ref[wr, rows, lanes], k_ref[wr, rows, lanes], v_ref[wr, rows, lanes],
                    bias, mask, mask_t, fold, heads,
                )[0].astype(BF16)

    xm_ref[...] = nn(gather[0], xw_ref[0]) + nn(gather[1], xw_ref[1]) + nn(gather[2], xw_ref[2])
    am_ref[...] = (
        nn(gather[0], att_ref[0]) + nn(gather[1], att_ref[1]) + nn(gather[2], att_ref[2])
    ).astype(BF16)

    @pl.loop(0, 4)
    def _(g):
        rows = pl.ds(pl.multiple_of(g * WINDOW, WINDOW), WINDOW)
        middle = xm_ref[rows, :] + nn(am_ref[rows, :], proj_one[...])
        normed = layer_norm(middle)[0].astype(BF16)
        active = gelu(nn(normed, up_one[...])).astype(BF16)
        one_ref[rows, :] = middle + nn(active, down_one[...])

    parts = [one_ref[g * WINDOW : (g + 1) * WINDOW, :] for g in range(4)]
    average = sum(jnp.sum(part, axis=-1, keepdims=True) for part in parts) / (4 * C1)
    spread_of = sum(
        jnp.sum((part - average) * (part - average), axis=-1, keepdims=True) for part in parts
    ) / (4 * C1)
    merge_scale = lax.rsqrt(spread_of + EPSILON)
    merged = [((part - average) * merge_scale) for part in parts]
    merged_low = [part.astype(BF16) for part in merged]
    grid = sum(nn(merged_low[g], merge[g * C1 : (g + 1) * C1, :]) for g in range(4))

    normed_full, scale = layer_norm(grid)
    normed = normed_full.astype(BF16)
    q, k, v = (nn(normed, qkv_two[:, j * C2 : (j + 1) * C2]).astype(BF16) for j in range(3))
    attended = []
    for index, (start, heads) in enumerate(GROUPS_TWO):
        lanes = slice(start * HEAD, (start + heads) * HEAD)
        taken, chances = attend(
            q[:, lanes], k[:, lanes], v[:, lanes], bias_two[index], mask, mask_t, fold, heads
        )
        p_ref[index] = chances
        attended.append(taken.astype(BF16))
    attended = jnp.concatenate(attended, axis=1)
    middle = grid + nn(attended, proj_two[...])
    normed_two_full, scale_two = layer_norm(middle)
    normed_two = normed_two_full.astype(BF16)
    active, slope = gelu_both(nn(normed_two, up_two[...]))
    active = active.astype(BF16)
    out_ref[...] = middle + nn(active, down_two[...])

    cot = []
    for r in range(3):
        value = cot_own[r].astype(F32)
        cot += [value[:, :C2], value[:, C2:]]
    for block in (right, up, diag):
        cot += rows_of(block, 9, 3)
    grad = nn(cot_select[...], jnp.concatenate(cot, axis=0).astype(BF16))
    grad_low = grad.astype(BF16)
    put(packed, 4608, tn(active, grad_low).astype(BF16))
    grad_raised = (nt(grad_low, down_two[...]) * slope).astype(BF16)
    put(packed, 0, tn(normed_two, grad_raised).astype(BF16))
    grad_middle = grad + layer_norm_back(nt(grad_raised, up_two[...]), normed_two_full, scale_two)
    grad_middle_low = grad_middle.astype(BF16)
    put(packed, 9216, tn(attended, grad_middle_low).astype(BF16))
    grad_attended = nt(grad_middle_low, proj_two[...]).astype(BF16)
    pieces = []
    for index, (start, heads) in enumerate(GROUPS_TWO):
        lanes = slice(start * HEAD, (start + heads) * HEAD)
        pieces.append(
            attend_back(
                q[:, lanes], k[:, lanes], v[:, lanes], p_ref[index], grad_attended[:, lanes],
                mask, mask_t, fold, heads,
            )
        )
    grad_normed = None
    for j in range(3):
        part = jnp.concatenate([piece[j].astype(BF16) for piece in pieces], axis=1)
        put(packed, 10368 + j * 1152, tn(normed, part).astype(BF16))
        term = nt(part, qkv_two[:, j * C2 : (j + 1) * C2])
        grad_normed = term if grad_normed is None else grad_normed + term
    grad_grid = (grad_middle + layer_norm_back(grad_normed, normed_full, scale)).astype(BF16)

    grad_parts = []
    grad_merge = [tn(merged_low[g], grad_grid).astype(BF16) for g in range(4)]
    put(packed, 13824, jnp.concatenate(grad_merge, axis=0))
    packed[1, 16128 - packed.shape[1] :, :] = jnp.zeros((256, LANES), BF16)
    for g in range(4):
        grad_parts.append(nt(grad_grid, merge[g * C1 : (g + 1) * C1, :]))
    first = sum(jnp.sum(part, axis=-1, keepdims=True) for part in grad_parts) / (4 * C1)
    second = sum(
        jnp.sum(part * kept, axis=-1, keepdims=True) for part, kept in zip(grad_parts, merged)
    ) / (4 * C1)
    for g in range(4):
        grad_ref[g * WINDOW : (g + 1) * WINDOW, :] = (
            merge_scale * (grad_parts[g] - first - merged[g] * second)
        ).astype(BF16)
    sent = nn(strips[...], grad_ref[...]).astype(BF16)
    lon_ref[...] = sent[: STRIPS[0]]
    lat_ref[...] = sent[STRIPS[0] : STRIPS[0] + STRIPS[1]]
    corner_ref[...] = sent[STRIPS[0] + STRIPS[1] :]
    send_halves(ids, packed, mine_ref, theirs_ref, sems)


def packed_shape(block):
    return jax.ShapeDtypeStruct((CHIPS * block, LANES), BF16)


def specs(count):
    vmem = pl.BlockSpec(memory_space=pltpu.VMEM)
    return [pl.BlockSpec(memory_space=pltpu.SMEM)] + [vmem] * (count - 1)


def out_specs(count, last_any):
    vmem, left = pl.BlockSpec(memory_space=pltpu.VMEM), pl.BlockSpec(memory_space=pl.ANY)
    return tuple([vmem] * (count - last_any) + [left] * last_any)


def upper(*operands):
    shape = jax.ShapeDtypeStruct
    return pl.pallas_call(
        upper_kernel,
        in_specs=specs(len(operands)),
        out_specs=out_specs(8, 2),
        out_shape=(
            shape((WINDOW, C2), F32),
            shape((3, 432, C1), BF16),
            shape((576, C1), BF16),
            shape((STRIPS[0], C1), BF16),
            shape((STRIPS[1], C1), BF16),
            shape((STRIPS[2], C1), BF16),
            packed_shape(UPPER_BLOCK),
            packed_shape(UPPER_BLOCK),
        ),
        scratch_shapes=[
            pltpu.VMEM((3, 432, C1), BF16),
            pltpu.VMEM((3, 432, C1), BF16),
            pltpu.VMEM((3, 432, C1), BF16),
            pltpu.VMEM((3, 432, C1), BF16),
            pltpu.VMEM((576, C1), F32),
            pltpu.VMEM((576, C1), BF16),
            pltpu.VMEM((576, C1), F32),
            pltpu.VMEM((3, WINDOW, 576), F32),
            pltpu.VMEM((2, CHIPS * UPPER_BLOCK, LANES), BF16),
            pltpu.SemaphoreType.DMA((2,)),
        ],
        compiler_params=pltpu.CompilerParams(vmem_limit_bytes=VMEM_BYTES),
        name="upper",
    )(*operands)


def lower_kernel(
    ids, xw, own, lon, lat, corner, bias_a, bias_b,
    qkv_one, proj_one, up_one, down_one,
    back_own, back_strips, mask_ref, mask_t_ref, fold_ref,
    out_ref, mine_ref, theirs_ref,
    gs_ref, normed_ref, full_ref, scale_ref, q_ref, k_ref, v_ref, pa_ref, pb_ref, att_ref,
    normed_two_ref, act_ref, raised_ref, gm_ref, gml_ref, gq_ref, gk_ref, gv_ref,
    packed, sems,
):
    mask, mask_t, fold = mask_ref[...], mask_t_ref[...], fold_ref[...]
    arrived = jnp.concatenate([lon[...], lat[...], corner[...]], axis=0)
    gs_ref[...] = nn(back_own[...], own[...]) + nn(back_strips[...], arrived)

    for row in range(2):
        rows = slice(row * 288, (row + 1) * 288)
        cells = xw[1 + row, :288, :].astype(F32)
        full, scale = layer_norm(cells)
        full_ref[rows, :] = full
        scale_ref[rows, :] = scale
        normed = full.astype(BF16)
        normed_ref[rows, :] = normed
        projected = nn(normed, qkv_one[...]).astype(BF16)
        q_ref[rows, :] = projected[:, :C1]
        k_ref[rows, :] = projected[:, C1 : 2 * C1]
        v_ref[rows, :] = projected[:, 2 * C1 :]

    @pl.loop(0, 2)
    def _(row):
        for wc in range(2):
            window = row * 2 + wc
            rows = pl.ds(pl.multiple_of(row * 288 + wc * WINDOW, WINDOW), WINDOW)
            for start, heads in GROUPS_ONE:
                lanes = slice(start * HEAD, (start + heads) * HEAD)
                bias = bias_a[1 + row] if heads == 4 else bias_b[1 + row]
                taken, chances = attend(
                    q_ref[rows, lanes], k_ref[rows, lanes], v_ref[rows, lanes],
                    bias, mask, mask_t, fold, heads,
                )
                att_ref[rows, lanes] = taken.astype(BF16)
                if heads == 4:
                    pa_ref[window] = chances
                else:
                    pb_ref[window] = chances

    @pl.loop(0, 4)
    def _(window):
        rows = pl.ds(pl.multiple_of(window * WINDOW, WINDOW), WINDOW)
        cells = xw[1 + window // 2, pl.ds(pl.multiple_of(window % 2 * WINDOW, WINDOW), WINDOW), :]
        middle = cells.astype(F32) + nn(att_ref[rows, :], proj_one[...])
        full, scale = layer_norm(middle)
        normed_two = full.astype(BF16)
        normed_two_ref[rows, :] = normed_two
        active, slope = gelu_both(nn(normed_two, up_one[...]))
        act_ref[rows, :] = active.astype(BF16)
        grad = gs_ref[rows, :]
        grad_raised = (nt(grad.astype(BF16), down_one[...]) * slope).astype(BF16)
        raised_ref[rows, :] = grad_raised
        grad_middle = grad + layer_norm_back(nt(grad_raised, up_one[...]), full, scale)
        gm_ref[rows, :] = grad_middle
        low = grad_middle.astype(BF16)
        gml_ref[rows, :] = low
        grad_attended = nt(low, proj_one[...]).astype(BF16)
        for start, heads in GROUPS_ONE:
            lanes = slice(start * HEAD, (start + heads) * HEAD)
            chances = pa_ref[window] if heads == 4 else pb_ref[window]
            gq, gk, gv = attend_back(
                q_ref[rows, lanes], k_ref[rows, lanes], v_ref[rows, lanes], chances,
                grad_attended[:, lanes], mask, mask_t, fold, heads,
            )
            gq_ref[rows, lanes] = gq.astype(BF16)
            gk_ref[rows, lanes] = gk.astype(BF16)
            gv_ref[rows, lanes] = gv.astype(BF16)
        grad_normed = (
            nt(gq_ref[rows, :], qkv_one[:, :C1])
            + nt(gk_ref[rows, :], qkv_one[:, C1 : 2 * C1])
            + nt(gv_ref[rows, :], qkv_one[:, 2 * C1 :])
        )
        out_ref[rows, :] = grad_middle + layer_norm_back(
            grad_normed, full_ref[rows, :], scale_ref[rows, :]
        )

    normed = normed_ref[...]
    grads = [tn(normed, ref[...]) for ref in (gq_ref, gk_ref, gv_ref)]
    grads = jnp.concatenate(grads + [tn(att_ref[...], gml_ref[...])], axis=1)
    put(packed, 0, grads.astype(BF16))
    put(packed, 1152, tn(normed_two_ref[...], raised_ref[...]).astype(BF16))
    low = gs_ref[...].astype(BF16)
    grads = [tn(act_ref[:, j * C1 : (j + 1) * C1], low) for j in range(4)]
    put(packed, 2304, jnp.concatenate(grads, axis=1).astype(BF16))
    packed[1, 3456 - packed.shape[1] :, :] = jnp.zeros((640, LANES), BF16)
    send_halves(ids, packed, mine_ref, theirs_ref, sems)


def lower(*operands):
    shape = jax.ShapeDtypeStruct
    wide = pltpu.VMEM((576, C1), BF16)
    return pl.pallas_call(
        lower_kernel,
        in_specs=specs(len(operands)),
        out_specs=out_specs(3, 2),
        out_shape=(
            shape((576, C1), F32), packed_shape(LOWER_BLOCK), packed_shape(LOWER_BLOCK)
        ),
        scratch_shapes=[
            pltpu.VMEM((576, C1), F32),
            wide,
            pltpu.VMEM((576, C1), F32),
            pltpu.VMEM((576, 1), F32),
            wide, wide, wide,
            pltpu.VMEM((4, WINDOW, 576), F32),
            pltpu.VMEM((4, WINDOW, 288), F32),
            wide,
            wide,
            pltpu.VMEM((576, 768), BF16),
            pltpu.VMEM((576, 768), BF16),
            pltpu.VMEM((576, C1), F32),
            wide, wide, wide, wide,
            pltpu.VMEM((2, CHIPS * LOWER_BLOCK, LANES), BF16),
            pltpu.SemaphoreType.DMA((2,)),
        ],
        compiler_params=pltpu.CompilerParams(vmem_limit_bytes=VMEM_BYTES),
        name="lower",
    )(*operands)


def call(kernel, name, out_shape, operands, scratch=()):
    return pl.pallas_call(
        kernel,
        in_specs=specs(len(operands)),
        out_shape=out_shape,
        scratch_shapes=scratch,
        compiler_params=pltpu.CompilerParams(vmem_limit_bytes=VMEM_BYTES),
        name=name,
    )(*operands)


def chip_kernel(ids, mine_two, theirs_two, mine_one, theirs_one, out):
    for low, mine, theirs in ((0, mine_two, theirs_two), (UPPER_BLOCK, mine_one, theirs_one)):
        rows = mine.shape[0] // CHIPS
        for block in range(CHIPS):
            at = slice(block * rows, (block + 1) * rows)
            value = mine[at].astype(F32) + theirs[at].astype(F32)
            out[block, low : low + rows, :] = value.astype(BF16)


def total_kernel(ids, blocks, out):
    value = blocks[0].astype(F32)
    for block in range(1, CHIPS):
        value = value + blocks[block].astype(F32)
    value = value.astype(BF16)
    for block in range(CHIPS):
        out[block] = value


def last_kernel(factor, ids, mine, theirs, qkv, proj, up, down, merge, qkv_two, proj_two, up_two, down_two, upper, lower):
    for half, source in ((ids[2], mine), (1 - ids[2], theirs)):
        for block in range(CHIPS):
            upper[half, block * UPPER_BLOCK : (block + 1) * UPPER_BLOCK, :] = source[block, :UPPER_BLOCK, :]
            lower[half, block * LOWER_BLOCK : (block + 1) * LOWER_BLOCK, :] = source[block, UPPER_BLOCK:, :]
    for out, base in ((up_two, 0), (down_two, 4608), (proj_two, 9216), (merge, 13824)):
        out[...] = take(upper, base, out.shape[0], out.shape[1] // LANES) * factor
    for j in range(3):
        qkv_two[:, j * C2 : (j + 1) * C2] = take(upper, 10368 + j * 1152, C2, 3) * factor
    joined = take(lower, 0, C1, 6) * factor
    qkv[...] = joined[:, : 3 * C1]
    proj[...] = joined[:, 3 * C1 :]
    up[...] = take(lower, 1152, C1, 6) * factor
    joined = take(lower, 2304, C1, 6) * factor
    for j in range(4):
        down[j * C1 : (j + 1) * C1, :] = joined[:, j * C1 : (j + 1) * C1]


def per_device(
    tokens, cotangent, bias_one, qkv_one, proj_one, up_one, down_one,
    merge_weight, bias_two, qkv_two, proj_two, up_two, down_two,
):
    lon = ("chip", "core")
    both = ("lat", "chip", "core")
    lats, lons = lax.axis_size("lat"), lax.axis_size(lon)
    ids = jnp.stack([lax.axis_index(name) for name in both]).astype(jnp.int32)
    factor = (WINDOW * lats * lons) ** -0.5
    from_right = [((i + 1) % lons, i) for i in range(lons)]
    to_right = [(i, (i + 1) % lons) for i in range(lons)]
    from_up = [(i, (i + 1) % lats) for i in range(lats)]
    to_up = [((i + 1) % lats, i) for i in range(lats)]
    other_core = [(i, 1 - i) for i in range(2)]
    corner_in = [
        (i * lons + (j + 1) % lons, (i + 1) % lats * lons + j) for i in range(lats) for j in range(lons)
    ]
    corner_out = [
        ((i + 1) % lats * lons + j, i * lons + (j + 1) % lons) for i in range(lats) for j in range(lons)
    ]
    for_left, for_down = pack(tokens[0], cotangent[0])
    right = lax.ppermute(for_left, lon, from_right)
    up = lax.ppermute(for_down, "lat", from_up)
    diag = lax.ppermute(for_down, both, corner_in)

    bias_a, bias_b, bias_c = expand_bias(ids, bias_one, bias_two, *bias_constants())
    select, gather, cot_select, strips, back_own, back_strips = constants()
    mask, mask_t, fold = blocks_of_heads()
    out_two, xw, grad_own, lon_strip, lat_strip, corner, mine_two, theirs_two = upper(
        ids, tokens[0], cotangent[0], right, up, diag, bias_a, bias_b, bias_c,
        qkv_one, proj_one, up_one, down_one, merge_weight, qkv_two, proj_two, up_two, down_two,
        select, gather, cot_select, strips, mask, mask_t, fold,
    )
    lon_strip = lax.ppermute(lon_strip, lon, to_right)
    lat_strip = lax.ppermute(lat_strip, "lat", to_up)
    corner = lax.ppermute(corner, both, corner_out)
    theirs_two = lax.ppermute(theirs_two, "core", other_core)
    grad_cells, mine_one, theirs_one = lower(
        ids, xw, grad_own, lon_strip, lat_strip, corner, bias_a, bias_b,
        qkv_one, proj_one, up_one, down_one,
        back_own, back_strips, mask, mask_t, fold,
    )
    theirs_one = lax.ppermute(theirs_one, "core", other_core)
    result = jax.ShapeDtypeStruct
    blocks = result((CHIPS, UPPER_BLOCK + LOWER_BLOCK, LANES), BF16)
    packed = call(chip_kernel, "chip", blocks, (ids, mine_two, theirs_two, mine_one, theirs_one))
    packed = lax.all_to_all(packed, ("lat", "chip"), 0, 0, tiled=True)
    packed = call(total_kernel, "total", blocks, (ids, packed))
    packed = lax.all_to_all(packed, ("lat", "chip"), 0, 0, tiled=True)
    weights = (
        qkv_one, proj_one, up_one, down_one, merge_weight, qkv_two, proj_two, up_two, down_two
    )
    sums = call(
        functools.partial(last_kernel, factor), "last", tuple(result(w.shape, F32) for w in weights),
        (ids, packed, lax.ppermute(packed, "core", other_core)),
        [
            pltpu.VMEM((2, CHIPS * UPPER_BLOCK, LANES), BF16),
            pltpu.VMEM((2, CHIPS * LOWER_BLOCK, LANES), BF16),
        ],
    )

    def shift_back(value, half_rows, half_cols):
        arrived = lax.ppermute(value[:, value.shape[1] - half_cols :], lon, to_right)
        value = jnp.concatenate([arrived, value[:, : value.shape[1] - half_cols]], axis=1)
        arrived = lax.ppermute(value[:half_rows], "lat", to_up)
        return jnp.concatenate([value[half_rows:], arrived], axis=0)

    out_two = out_two.reshape(12, LEVELS, WLAT, C2).transpose(2, 0, 1, 3).reshape(6, 12, LEVELS * C2)
    out_two = shift_back(out_two, WLAT // 2, WLON // 2)[None]
    grad_cells = grad_cells.reshape(2, 24, LEVELS, WLAT, C1).transpose(0, 3, 1, 2, 4)
    grad_tokens = shift_back(grad_cells.reshape(12, 24, LEVELS * C1), WLAT // 2, WLON // 2)[None]
    return (out_two, grad_tokens, *sums)


def solution(mesh):
    lats, lons = mesh.devices.shape
    mesh = Mesh(mesh.devices.reshape(lats, lons // 2, 2), ("lat", "chip", "core"))
    sharded, copied = P(None, "lat", ("chip", "core"), None), P()
    return jax.shard_map(
        per_device,
        mesh=mesh,
        in_specs=(sharded, sharded) + (copied,) * 11,
        out_specs=(sharded, sharded) + (copied,) * 9,
        check_vma=False,
    )
```

```python
import functools

import jax
import jax.numpy as jnp
import numpy as np
from jax import lax
from jax.experimental import pallas as pl
from jax.experimental.pallas import tpu as pltpu
from jax.sharding import Mesh, PartitionSpec as P

C1 = 192
C2 = 384
HEAD = 32
LEVELS = 2
WLAT = 6
WLON = 12
WINDOW = 144
REL = 2 * WLON - 1
COLUMN = LEVELS * WLAT
FACTOR = HEAD**-0.5
EPSILON = 1e-05
MASKED = -1e30
GROUPS_ONE = ((0, 4), (4, 2))
GROUPS_TWO = ((0, 4), (4, 4), (8, 4))
STRIPS = (112, 112, 48)
MIB = 1024 * 1024
SHIFT = (96, 96, 64)
SHIFT_TOKENS = (56, 56, 24)
LANES = 128
CHIPS = 64
UPPER_BLOCK = 128
LOWER_BLOCK = 32
F32 = jnp.float32
BF16 = jnp.bfloat16


def constants():
    select = np.zeros((2, 432, 288), np.float32)
    for col in range(36):
        half, source = (0, 6 + col) if col < 18 else (1, col - 18)
        for level in range(2):
            for a in range(6):
                select[level, col * 12 + level * 6 + a, half * 144 + a * 24 + source] = 1
    own = {}
    gather = np.zeros((3, 576, 432), np.float32)
    for pr in range(2):
        for pc in range(2):
            for out_col in range(12):
                for level in range(2):
                    for out_row in range(6):
                        row, col = 3 + 2 * out_row + pr, 6 + 2 * out_col + pc
                        place = (pr * 2 + pc) * 144 + out_col * 12 + level * 6 + out_row
                        gather[row // 6, place, col * 12 + level * 6 + row % 6] = 1
                        own[row, col, level] = place
    cot_select = np.zeros((144, 288), np.float32)
    for out_col in range(12):
        for out_row in range(6):
            for level in range(2):
                up, right = out_row < 3, out_col >= 6
                block = (2 if up else 0) + (1 if right else 0)
                col = out_col - 6 if right else 6 + out_col
                place = out_col * 12 + level * 6 + out_row
                cot_select[place, block * 72 + out_row % 3 * 24 + level * 12 + col] = 1
    strips = np.zeros((sum(STRIPS), 576), np.float32)
    back_own = np.zeros((576, 576), np.float32)
    back_strips = np.zeros((576, sum(STRIPS)), np.float32)
    for row in range(6, 18):
        for col in range(24):
            for level in range(2):
                target = (row - 6) // 6 * 288 + col * 12 + level * 6 + row % 6
                if row <= 14 and col >= 6:
                    back_own[target, own[row, col, level]] = 1
                    continue
                if row <= 14:
                    place = (row - 6) * 12 + col * 2 + level
                    sent = (row, 24 + col, level)
                elif col >= 6:
                    place = STRIPS[0] + (row - 15) * 36 + (col - 6) * 2 + level
                    sent = (row - 12, col, level)
                else:
                    place = STRIPS[0] + STRIPS[1] + (row - 15) * 12 + col * 2 + level
                    sent = (row - 12, 24 + col, level)
                back_strips[target, place] = 1
                strips[place, own[sent]] = 1
    return tuple(jnp.asarray(v, BF16) for v in (select, gather, cot_select, strips, back_own, back_strips))


def output_constants():
    starts = (0, SHIFT[0], SHIFT[0] + SHIFT[1])
    tokens = np.zeros((2, 288 + sum(SHIFT_TOKENS), 576), np.float32)
    place = np.zeros((288, sum(SHIFT)), np.float32)
    two = np.zeros((144 + sum(SHIFT) - sum(SHIFT_TOKENS), WINDOW), np.float32)
    place_two = np.zeros((144, sum(SHIFT)), np.float32)

    def strip(row, col, rows, cols):
        if row < rows:
            return (None, row, col - cols) if col >= cols else (0, row, col)
        return (1, row - rows, col - cols) if col >= cols else (2, row - rows, col)

    for row in range(12):
        for col in range(24):
            kind, sub_row, sub_col = strip(row, col, 9, 6)
            source_row = row + 3 if row < 9 else row - 9
            source_col = col - 6 if col >= 6 else col + 18
            if kind is None:
                target = row * 24 + col
            else:
                at = sub_row * (18 if kind == 1 else 6) + sub_col
                target = 288 + sum(SHIFT_TOKENS[:kind]) + at
                place[row * 24 + col, starts[kind] + at] = 1
            for level in range(2):
                source = source_row // 6 * 288 + source_col * 12 + level * 6 + source_row % 6
                tokens[level, target, source] = 1
    for row in range(6):
        for col in range(12):
            kind, sub_row, sub_col = strip(row, col, 3, 6)
            source_row = row + 3 if row < 3 else row - 3
            source_col = col - 6 if col >= 6 else col + 6
            for level in range(2):
                if kind is None:
                    target = level * 72 + row * 12 + col
                else:
                    at = level * 18 + sub_row * 6 + sub_col
                    target = 144 + kind * 40 + at
                    place_two[level * 72 + row * 12 + col, starts[kind] + SHIFT_TOKENS[kind] + at] = 1
                two[target, source_col * 12 + level * 6 + source_row] = 1
    return tuple(jnp.asarray(v, BF16) for v in (tokens, two, place, place_two))


def bias_constants():
    z1, z2, a1, a2, r = (v.reshape(-1) for v in np.indices((LEVELS, LEVELS, WLAT, WLAT, REL)))
    half = WLAT // 2
    kind = np.where((a1 < half) & (a2 < half), 0.0, np.where((a1 >= half) & (a2 >= half), 1.0, 2.0))
    rows = np.stack(
        [(z2 == level)[None] & (a2[None] + 2 * (1 - level) == np.arange(8)[:, None]) for level in range(2)]
    )
    lanes = (r * COLUMN + z1 * WLAT + a1)[:, None] == np.arange(REL * COLUMN)[None]
    return (
        jnp.asarray(kind[None], F32),
        jnp.asarray(rows, F32),
        jnp.asarray(lanes.astype(np.float32), BF16),
    )


def blocks_of_heads():
    mask = (np.arange(576)[:, None] // WINDOW == np.arange(128)[None] // HEAD).astype(np.float32)
    fold = (np.arange(WINDOW)[:, None] == np.arange(576)[None] % WINDOW).astype(np.float32)
    return tuple(jnp.asarray(v, BF16) for v in (mask, mask.T, fold))


def params(microseconds, vmem):
    return {
        "compiler_params": pltpu.CompilerParams(vmem_limit_bytes=vmem * MIB),
        "cost_estimate": pl.CostEstimate(
            flops=int(microseconds * 1e9), bytes_accessed=int(microseconds * 3e6), transcendentals=0
        ),
    }


def nn(left, right):
    return jnp.dot(left, right, preferred_element_type=F32)


def nt(left, right):
    return lax.dot_general(left, right, (((1,), (1,)), ((), ())), preferred_element_type=F32)


def tn(left, right):
    return lax.dot_general(left, right, (((0,), (0,)), ((), ())), preferred_element_type=F32)


def layer_norm(values):
    average = jnp.mean(values, axis=-1, keepdims=True)
    centred = values - average
    scale = lax.rsqrt(jnp.mean(centred * centred, axis=-1, keepdims=True) + EPSILON)
    return centred * scale, scale


def layer_norm_back(grad, normed, scale):
    first = jnp.mean(grad, axis=-1, keepdims=True)
    second = jnp.mean(grad * normed, axis=-1, keepdims=True)
    return scale * (grad - first - normed * second)


GELU_A = (2.0 / np.pi) ** 0.5
GELU_B = 0.044715


def gelu(values):
    tanh = jnp.tanh(GELU_A * (values + GELU_B * (values * values * values)))
    return 0.5 * values * (1.0 + tanh)


def gelu_both(values):
    square = values * values
    tanh = jnp.tanh(GELU_A * values * (1.0 + GELU_B * square))
    half = 0.5 * (1.0 + tanh)
    slope = half + 0.5 * values * (1.0 - tanh * tanh) * (GELU_A * (1.0 + 3.0 * GELU_B * square))
    return values * half, slope


def spread(values, mask, heads):
    return jnp.concatenate([values] * heads, axis=0) * mask[: heads * WINDOW, : heads * HEAD]


def pull(left, right, mask_t, fold, heads):
    both = tn(left, right).astype(BF16) * mask_t[: heads * HEAD, : heads * WINDOW]
    return nt(fold[:, : heads * WINDOW], both)


def attend(parts, mask, mask_t, fold):
    scores = [
        nt(keys, spread(queries, mask, heads)) * FACTOR + bias for queries, keys, _, bias, heads in parts
    ]
    powers = [jnp.exp(score - jnp.max(score, axis=0, keepdims=True)) for score in scores]
    chances = [power * (1.0 / jnp.sum(power, axis=0, keepdims=True)) for power in powers]
    taken = [
        pull(part[2], chance.astype(BF16), mask_t, fold, part[4]) for part, chance in zip(parts, chances)
    ]
    return taken, chances


def attend_back(parts, mask, mask_t, fold):
    grads = [spread(part[4], mask, part[5]) for part in parts]
    grad_chances = [nt(part[2], grad) for part, grad in zip(parts, grads)]
    grad_values = [nn(part[3].astype(BF16), grad) for part, grad in zip(parts, grads)]
    products = [grad * part[3] for part, grad in zip(parts, grad_chances)]
    grad_scores = [
        ((product - part[3] * jnp.sum(product, axis=0, keepdims=True)) * FACTOR).astype(BF16)
        for part, product in zip(parts, products)
    ]
    grad_keys = [nn(grad, spread(part[0], mask, part[5])) for part, grad in zip(parts, grad_scores)]
    grad_queries = [
        pull(part[1], grad, mask_t, fold, part[5]) for part, grad in zip(parts, grad_scores)
    ]
    return grad_queries, grad_keys, grad_values


SPANS = (((0, 896), (1536, 2560)), ((768, 1664), (2432, 3312)))


def bias_kernel(ids, one, two, kind, rows, lanes, first_ref, second_ref, two_out_ref, pieces, table):
    band = ids[0]

    def window(source, index):
        count = source.shape[0] - 1
        index = lax.rem(index + count, count)
        mixed = jnp.where(
            kind[...] == 0.0, source[count], jnp.where(kind[...] == 1.0, source[0], MASKED)
        )
        return jnp.where(index == 0, mixed, source[index])

    values = [
        window(one, 2 * band - 1), window(one, 2 * band), window(one, 2 * band + 1), window(two, band)
    ]
    heads = sum(value.shape[0] for value in values)
    for level in range(2):
        slot = 0
        for value in values:
            high = value.astype(BF16).astype(F32)
            low = value - high
            for h in range(0, value.shape[0], 2):
                for piece, taken in enumerate((high, low)):
                    at = 0
                    for start, stop in SPANS[level]:
                        chosen = rows[level, :, start:stop] > 0.0
                        pair = [
                            jnp.where(chosen, taken[h + i : h + i + 1, start:stop], 0.0) for i in range(2)
                        ]
                        pieces[piece, (slot + h) * 8 : (slot + h) * 8 + 16, at : at + stop - start] = (
                            jnp.concatenate(pair, axis=0).astype(BF16)
                        )
                        at += stop - start
            slot += value.shape[0]
        total = None
        for piece in range(2):
            at = 0
            for start, stop in SPANS[level]:
                term = nn(pieces[piece, :, at : at + stop - start], lanes[start:stop, :])
                total = term if total is None else total + term
                at += stop - start
        for h in range(heads):
            table[h, level * 8 : level * 8 + 8, :] = total[h * 8 : h * 8 + 8]

    for base, count, groups, targets in (
        (0, 3, GROUPS_ONE, (first_ref, second_ref)),
        (18, 1, GROUPS_TWO, (two_out_ref, two_out_ref, two_out_ref)),
    ):
        for row in range(count):
            for index, (start, heads) in enumerate(groups):
                target = targets[index]
                place = row if count == 3 else index
                which = [base + row * 6 + start + h for h in range(heads)]
                for o2 in range(WLON):
                    left = (WLON - 1 - o2) * COLUMN
                    piece = [table[h, 2 : 2 + COLUMN, left : left + WINDOW] for h in which]
                    target[place, o2 * COLUMN : (o2 + 1) * COLUMN, :] = jnp.concatenate(piece, axis=1)


def expand_bias(*operands):
    return pl.pallas_call(
        bias_kernel,
        in_specs=specs(len(operands)),
        out_shape=(
            jax.ShapeDtypeStruct((3, WINDOW, 576), F32),
            jax.ShapeDtypeStruct((3, WINDOW, 288), F32),
            jax.ShapeDtypeStruct((3, WINDOW, 576), F32),
        ),
        scratch_shapes=[
            pltpu.VMEM((2, 240, 1920), BF16),
            pltpu.VMEM((30, 16, REL * COLUMN), F32),
        ],
        **params(7, 24),
        name="bias_expand",
    )(*operands)


def pack_kernel(tokens, cot, right_ref, up_ref):
    for out, row, cot_row in ((right_ref, 0, 0), (up_ref, 3, 3)):
        out[:9] = tokens[row : row + 9]
        for r in range(3):
            value = cot[cot_row + r].astype(F32)
            out[9 + r] = jnp.concatenate([value[:, :C2], value[:, C2:]], axis=0).astype(BF16)


def pack(tokens, cot):
    shape = jax.ShapeDtypeStruct((12, 24, 2 * C1), BF16)
    return pl.pallas_call(
        pack_kernel, out_shape=(shape, shape), name="pack", **params(2, 8)
    )(tokens, cot)


def put(packed, base, value):
    half, count = packed.shape[1], value.shape[0]
    for j in range(value.shape[1] // LANES):
        start, stop = base + j * count, base + (j + 1) * count
        lanes = value[:, j * LANES : (j + 1) * LANES]
        for part in range(2):
            low, high = max(start, part * half), min(stop, (part + 1) * half)
            if low < high:
                packed[part, low - part * half : high - part * half, :] = lanes[low - start : high - start]
    return base + value.shape[0] * value.shape[1] // LANES


def take(packed, base, count, columns):
    half, lanes = packed.shape[1], []
    for j in range(columns):
        start, stop, rows = base + j * count, base + (j + 1) * count, []
        for part in range(2):
            low, high = max(start, part * half), min(stop, (part + 1) * half)
            if low < high:
                rows.append(packed[part, low - part * half : high - part * half, :])
        lanes.append(rows[0] if len(rows) == 1 else jnp.concatenate(rows, axis=0))
    return jnp.concatenate(lanes, axis=1).astype(F32)


def send_half(ids, packed, half, mine_ref, theirs_ref, sems, start):
    for target, own in ((mine_ref, half), (theirs_ref, 1 - half)):

        @pl.when(ids[2] == own)
        def _():
            copy = pltpu.make_async_copy(packed.at[half], target, sems.at[half])
            if start:
                copy.start()
            else:
                copy.wait()


def upper_kernel(
    ids, own, cot_own, right, up, diag,
    bias_a, bias_b, bias_two,
    qkv_one, proj_one, up_one, down_one, merge, qkv_two, proj_two, up_two, down_two,
    select, gather, cot_select, strips, mask_ref, mask_t_ref, fold_ref,
    out_ref, xw_ref, grad_ref, lon_ref, lat_ref, corner_ref, mine_ref, theirs_ref,
    q_ref, k_ref, v_ref, att_ref, xm_ref, am_ref, one_ref, p_ref, packed, sems,
):
    mask, mask_t, fold = mask_ref[...], mask_t_ref[...], fold_ref[...]

    def rows_of(block, start, count):
        return [block[start + r].astype(F32) for r in range(count)]

    for wr in range(3):
        if wr == 0:
            left, other = rows_of(up, 0, 6), rows_of(diag, 0, 6)
        elif wr == 1:
            left = rows_of(up, 6, 3) + rows_of(own, 0, 3)
            other = rows_of(diag, 6, 3) + rows_of(right, 0, 3)
        else:
            left, other = rows_of(own, 3, 6), rows_of(right, 3, 6)
        source = jnp.concatenate(left + other, axis=0).astype(BF16)
        cells = nn(select[0], source[:, :C1]) + nn(select[1], source[:, C1:])
        xw_ref[wr] = cells.astype(BF16)
        normed = layer_norm(cells)[0].astype(BF16)
        projected = nn(normed, qkv_one[...]).astype(BF16)
        q_ref[wr] = projected[:, :C1]
        k_ref[wr] = projected[:, C1 : 2 * C1]
        v_ref[wr] = projected[:, 2 * C1 :]

    @pl.loop(0, 3)
    def _(wr):
        places = [
            (slice(wc * WINDOW, (wc + 1) * WINDOW), slice(start * HEAD, (start + heads) * HEAD), heads)
            for wc in range(3)
            for start, heads in GROUPS_ONE
        ]
        parts = [
            (
                q_ref[wr, rows, lanes], k_ref[wr, rows, lanes], v_ref[wr, rows, lanes],
                bias_a[wr] if heads == 4 else bias_b[wr], heads,
            )
            for rows, lanes, heads in places
        ]
        taken, _ = attend(parts, mask, mask_t, fold)
        for (rows, lanes, heads), value in zip(places, taken):
            att_ref[wr, rows, lanes] = value.astype(BF16)

    xm_ref[...] = nn(gather[0], xw_ref[0]) + nn(gather[1], xw_ref[1]) + nn(gather[2], xw_ref[2])
    am_ref[...] = (
        nn(gather[0], att_ref[0]) + nn(gather[1], att_ref[1]) + nn(gather[2], att_ref[2])
    ).astype(BF16)

    for half in range(2):
        rows = slice(half * 288, (half + 1) * 288)
        middle = xm_ref[rows, :] + nn(am_ref[rows, :], proj_one[...])
        normed = layer_norm(middle)[0].astype(BF16)
        active = gelu(nn(normed, up_one[...])).astype(BF16)
        one_ref[rows, :] = middle + nt(active, down_one[...])

    parts = [one_ref[g * WINDOW : (g + 1) * WINDOW, :] for g in range(4)]
    average = sum(jnp.sum(part, axis=-1, keepdims=True) for part in parts) / (4 * C1)
    spread_of = sum(
        jnp.sum((part - average) * (part - average), axis=-1, keepdims=True) for part in parts
    ) / (4 * C1)
    merge_scale = lax.rsqrt(spread_of + EPSILON)
    merged = [((part - average) * merge_scale) for part in parts]
    merged_low = [part.astype(BF16) for part in merged]
    grid = sum(nn(merged_low[g], merge[g * C1 : (g + 1) * C1, :]) for g in range(4))

    normed_full, scale = layer_norm(grid)
    normed = normed_full.astype(BF16)
    q, k, v = (nn(normed, qkv_two[:, j * C2 : (j + 1) * C2]).astype(BF16) for j in range(3))
    lanes_of = [slice(start * HEAD, (start + heads) * HEAD) for start, heads in GROUPS_TWO]
    taken, chances = attend(
        [(q[:, at], k[:, at], v[:, at], bias_two[index], 4) for index, at in enumerate(lanes_of)],
        mask, mask_t, fold,
    )
    for index in range(3):
        p_ref[index] = chances[index]
    attended = jnp.concatenate([value.astype(BF16) for value in taken], axis=1)
    middle = grid + nn(attended, proj_two[...])
    normed_two_full, scale_two = layer_norm(middle)
    normed_two = normed_two_full.astype(BF16)
    active, slope = gelu_both(nn(normed_two, up_two[...]))
    active = active.astype(BF16)
    out_ref[...] = middle + nn(active, down_two[...])

    cot = []
    for r in range(3):
        value = cot_own[r].astype(F32)
        cot += [value[:, :C2], value[:, C2:]]
    for block in (right, up, diag):
        cot += rows_of(block, 9, 3)
    grad = nn(cot_select[...], jnp.concatenate(cot, axis=0).astype(BF16))
    grad_low = grad.astype(BF16)
    put(packed, 4608, tn(active, grad_low).astype(BF16))
    grad_raised = (nt(grad_low, down_two[...]) * slope).astype(BF16)
    put(packed, 0, tn(normed_two, grad_raised).astype(BF16))
    send_half(ids, packed, 0, mine_ref, theirs_ref, sems, True)
    grad_middle = grad + layer_norm_back(nt(grad_raised, up_two[...]), normed_two_full, scale_two)
    grad_middle_low = grad_middle.astype(BF16)
    put(packed, 9216, tn(attended, grad_middle_low).astype(BF16))
    grad_attended = nt(grad_middle_low, proj_two[...]).astype(BF16)
    pieces = attend_back(
        [
            (q[:, at], k[:, at], v[:, at], p_ref[index], grad_attended[:, at], 4)
            for index, at in enumerate(lanes_of)
        ],
        mask, mask_t, fold,
    )
    grad_normed = None
    for j in range(3):
        part = jnp.concatenate([value.astype(BF16) for value in pieces[j]], axis=1)
        put(packed, 10368 + j * 1152, tn(normed, part).astype(BF16))
        term = nt(part, qkv_two[:, j * C2 : (j + 1) * C2])
        grad_normed = term if grad_normed is None else grad_normed + term
    grad_grid = (grad_middle + layer_norm_back(grad_normed, normed_full, scale)).astype(BF16)

    grad_parts = []
    grad_merge = [tn(merged_low[g], grad_grid).astype(BF16) for g in range(4)]
    put(packed, 13824, jnp.concatenate(grad_merge, axis=0))
    packed[1, 16128 - packed.shape[1] :, :] = jnp.zeros((256, LANES), BF16)
    send_half(ids, packed, 1, mine_ref, theirs_ref, sems, True)
    for g in range(4):
        grad_parts.append(nt(grad_grid, merge[g * C1 : (g + 1) * C1, :]))
    first = sum(jnp.sum(part, axis=-1, keepdims=True) for part in grad_parts) / (4 * C1)
    second = sum(
        jnp.sum(part * kept, axis=-1, keepdims=True) for part, kept in zip(grad_parts, merged)
    ) / (4 * C1)
    for g in range(4):
        grad_ref[g * WINDOW : (g + 1) * WINDOW, :] = (
            merge_scale * (grad_parts[g] - first - merged[g] * second)
        ).astype(BF16)
    sent = nn(strips[...], grad_ref[...]).astype(BF16)
    lon_ref[...] = sent[: STRIPS[0]]
    lat_ref[...] = sent[STRIPS[0] : STRIPS[0] + STRIPS[1]]
    corner_ref[...] = sent[STRIPS[0] + STRIPS[1] :]
    for half in range(2):
        send_half(ids, packed, half, mine_ref, theirs_ref, sems, False)


def packed_shape(block):
    return jax.ShapeDtypeStruct((CHIPS * block, LANES), BF16)


def specs(count):
    vmem = pl.BlockSpec(memory_space=pltpu.VMEM)
    return [pl.BlockSpec(memory_space=pltpu.SMEM)] + [vmem] * (count - 1)


def out_specs(count, last_any):
    vmem, left = pl.BlockSpec(memory_space=pltpu.VMEM), pl.BlockSpec(memory_space=pl.ANY)
    return tuple([vmem] * (count - last_any) + [left] * last_any)


def upper(*operands):
    shape = jax.ShapeDtypeStruct
    return pl.pallas_call(
        upper_kernel,
        in_specs=specs(len(operands)),
        out_specs=out_specs(8, 2),
        out_shape=(
            shape((WINDOW, C2), F32),
            shape((3, 432, C1), BF16),
            shape((576, C1), BF16),
            shape((STRIPS[0], C1), BF16),
            shape((STRIPS[1], C1), BF16),
            shape((STRIPS[2], C1), BF16),
            packed_shape(UPPER_BLOCK),
            packed_shape(UPPER_BLOCK),
        ),
        scratch_shapes=[
            pltpu.VMEM((3, 432, C1), BF16),
            pltpu.VMEM((3, 432, C1), BF16),
            pltpu.VMEM((3, 432, C1), BF16),
            pltpu.VMEM((3, 432, C1), BF16),
            pltpu.VMEM((576, C1), F32),
            pltpu.VMEM((576, C1), BF16),
            pltpu.VMEM((576, C1), F32),
            pltpu.VMEM((3, WINDOW, 576), F32),
            pltpu.VMEM((2, CHIPS * UPPER_BLOCK, LANES), BF16),
            pltpu.SemaphoreType.DMA((2,)),
        ],
        **params(25, 40),
        name="upper",
    )(*operands)


def halves(value):
    high = value.astype(BF16)
    return high, (value - high.astype(F32)).astype(BF16)


def lower_kernel(
    ids, xw, out_two, own, lon, lat, corner, bias_a, bias_b,
    qkv_one, proj_one, up_one, down_one,
    back_own, back_strips, to_tokens, to_two, mask_ref, mask_t_ref, fold_ref,
    out_ref, out_two_ref, lon_ref, lat_ref, corner_ref, mine_ref, theirs_ref,
    gs_ref, normed_ref, full_ref, scale_ref, q_ref, k_ref, v_ref, pa_ref, pb_ref, att_ref,
    normed_two_ref, act_ref, raised_ref, gm_ref, gml_ref, ga_ref, gq_ref, gk_ref, gv_ref, gx_ref,
    packed, sems,
):
    mask, mask_t, fold = mask_ref[...], mask_t_ref[...], fold_ref[...]
    arrived = jnp.concatenate([lon[...], lat[...], corner[...]], axis=0)
    gs_ref[...] = nn(back_own[...], own[...]) + nn(back_strips[...], arrived)
    row_slices = [slice(row * 288, (row + 1) * 288) for row in range(2)]

    for row, rows in enumerate(row_slices):
        full, scale = layer_norm(xw[1 + row, :288, :].astype(F32))
        full_ref[rows, :] = full
        scale_ref[rows, :] = scale
        normed = full.astype(BF16)
        normed_ref[rows, :] = normed
        projected = nn(normed, qkv_one[...]).astype(BF16)
        q_ref[rows, :] = projected[:, :C1]
        k_ref[rows, :] = projected[:, C1 : 2 * C1]
        v_ref[rows, :] = projected[:, 2 * C1 :]

    def places(row):
        return [
            (
                pl.ds(pl.multiple_of(row * 288 + wc * WINDOW, WINDOW), WINDOW),
                slice(start * HEAD, (start + heads) * HEAD),
                heads,
                (pa_ref if heads == 4 else pb_ref, row * 2 + wc),
                bias_a if heads == 4 else bias_b,
            )
            for wc in range(2)
            for start, heads in GROUPS_ONE
        ]

    @pl.loop(0, 2)
    def _(row):
        parts = [
            (q_ref[rows, at], k_ref[rows, at], v_ref[rows, at], bias[1 + row], heads)
            for rows, at, heads, _, bias in places(row)
        ]
        taken, chances = attend(parts, mask, mask_t, fold)
        for (rows, at, _, (kept, window), _), value, chance in zip(places(row), taken, chances):
            att_ref[rows, at] = value.astype(BF16)
            kept[window] = chance

    for row, rows in enumerate(row_slices):
        middle = xw[1 + row, :288, :].astype(F32) + nn(att_ref[rows, :], proj_one[...])
        full, scale = layer_norm(middle)
        normed_two = full.astype(BF16)
        normed_two_ref[rows, :] = normed_two
        active, slope = gelu_both(nn(normed_two, up_one[...]))
        act_ref[rows, :] = active.astype(BF16)
        grad = gs_ref[rows, :]
        grad_raised = (nn(grad.astype(BF16), down_one[...]) * slope).astype(BF16)
        raised_ref[rows, :] = grad_raised
        grad_middle = grad + layer_norm_back(nt(grad_raised, up_one[...]), full, scale)
        gm_ref[rows, :] = grad_middle
        low = grad_middle.astype(BF16)
        gml_ref[rows, :] = low
        ga_ref[rows, :] = nt(low, proj_one[...]).astype(BF16)

    @pl.loop(0, 2)
    def _(row):
        parts = [
            (q_ref[rows, at], k_ref[rows, at], v_ref[rows, at], kept[window], ga_ref[rows, at], heads)
            for rows, at, heads, (kept, window), _ in places(row)
        ]
        grads = attend_back(parts, mask, mask_t, fold)
        for target, values in zip((gq_ref, gk_ref, gv_ref), grads):
            for (rows, at, _, _, _), value in zip(places(row), values):
                target[rows, at] = value.astype(BF16)

    normed = normed_ref[...]
    grads = [tn(normed, ref[...]) for ref in (gq_ref, gk_ref, gv_ref)]
    grads = jnp.concatenate(grads + [tn(att_ref[...], gml_ref[...])], axis=1)
    put(packed, 0, grads.astype(BF16))
    put(packed, 1152, tn(normed_two_ref[...], raised_ref[...]).astype(BF16))
    put(packed, 2304, tn(gs_ref[...].astype(BF16), act_ref[...]).astype(BF16))
    packed[1, 3456 - packed.shape[1] :, :] = jnp.zeros((640, LANES), BF16)
    for half in range(2):
        send_half(ids, packed, half, mine_ref, theirs_ref, sems, True)

    for rows in row_slices:
        grad_normed = (
            nt(gq_ref[rows, :], qkv_one[:, :C1])
            + nt(gk_ref[rows, :], qkv_one[:, C1 : 2 * C1])
            + nt(gv_ref[rows, :], qkv_one[:, 2 * C1 :])
        )
        gx_ref[rows, :] = gm_ref[rows, :] + layer_norm_back(
            grad_normed, full_ref[rows, :], scale_ref[rows, :]
        )
    high, low = halves(gx_ref[...])
    cells = jnp.concatenate(
        [nn(to_tokens[level], high) + nn(to_tokens[level], low) for level in range(2)], axis=1
    )
    high, low = halves(out_two[...])
    two = nn(to_two[...], high) + nn(to_two[...], low)
    out_ref[...] = cells[:288]
    out_two_ref[...] = two[:144]
    at = 288
    for kind, ref in enumerate((lon_ref, lat_ref, corner_ref)):
        count = SHIFT_TOKENS[kind]
        ref[:count, :] = cells[at : at + count]
        ref[count:, :] = two[144 + kind * 40 : 144 + (kind + 1) * 40]
        at += count
    for half in range(2):
        send_half(ids, packed, half, mine_ref, theirs_ref, sems, False)


def lower(*operands):
    shape = jax.ShapeDtypeStruct
    wide = pltpu.VMEM((576, C1), BF16)
    return pl.pallas_call(
        lower_kernel,
        in_specs=specs(len(operands)),
        out_specs=out_specs(7, 2),
        out_shape=(
            shape((288, C2), F32),
            shape((144, C2), F32),
            *(shape((count, C2), F32) for count in SHIFT),
            packed_shape(LOWER_BLOCK),
            packed_shape(LOWER_BLOCK),
        ),
        scratch_shapes=[
            pltpu.VMEM((576, C1), F32),
            wide,
            pltpu.VMEM((576, C1), F32),
            pltpu.VMEM((576, 1), F32),
            wide, wide, wide,
            pltpu.VMEM((4, WINDOW, 576), F32),
            pltpu.VMEM((4, WINDOW, 288), F32),
            wide,
            wide,
            pltpu.VMEM((576, 768), BF16),
            pltpu.VMEM((576, 768), BF16),
            pltpu.VMEM((576, C1), F32),
            wide, wide, wide, wide, wide,
            pltpu.VMEM((576, C1), F32),
            pltpu.VMEM((2, CHIPS * LOWER_BLOCK, LANES), BF16),
            pltpu.SemaphoreType.DMA((2,)),
        ],
        **params(15, 60),
        name="lower",
    )(*operands)


def call(kernel, name, microseconds, vmem, out_shape, operands, scratch=()):
    return pl.pallas_call(
        kernel,
        in_specs=specs(len(operands)),
        out_shape=out_shape,
        scratch_shapes=scratch,
        name=name,
        **params(microseconds, vmem),
    )(*operands)


def chip_kernel(ids, mine, theirs, out):
    rows = out.shape[1]
    for block in range(CHIPS):
        at = slice(block * rows, (block + 1) * rows)
        out[block] = (mine[at].astype(F32) + theirs[at].astype(F32)).astype(BF16)


def total(blocks, low, rows):
    value = blocks[0, low : low + rows, :].astype(F32)
    for block in range(1, CHIPS):
        value = value + blocks[block, low : low + rows, :].astype(F32)
    return value.astype(BF16)


def middle_kernel(ids, blocks, packed_one, out):
    value = total(blocks, 0, UPPER_BLOCK)
    for block in range(CHIPS):
        out[block, :UPPER_BLOCK, :] = value
        out[block, UPPER_BLOCK:, :] = packed_one[block]


def total_kernel(ids, blocks, out):
    value = total(blocks, UPPER_BLOCK, LOWER_BLOCK)
    for block in range(CHIPS):
        out[block] = value


def join_halves(ids, mine, theirs, packed):
    rows = packed.shape[1] // CHIPS
    for half, source in ((ids[2], mine), (1 - ids[2], theirs)):
        for block in range(CHIPS):
            packed[half, block * rows : (block + 1) * rows, :] = source[block, :rows, :]


def upper_last_kernel(factor, ids, mine, theirs, merge, qkv, proj, up, down, packed):
    join_halves(ids, mine, theirs, packed)
    for out, base in ((up, 0), (down, 4608), (proj, 9216), (merge, 13824)):
        out[...] = take(packed, base, out.shape[0], out.shape[1] // LANES) * factor
    for j in range(3):
        qkv[:, j * C2 : (j + 1) * C2] = take(packed, 10368 + j * 1152, C2, 3) * factor


def lower_last_kernel(factor, ids, mine, theirs, qkv, proj, up, down, packed):
    join_halves(ids, mine, theirs, packed)
    joined = take(packed, 0, C1, 6) * factor
    qkv[...] = joined[:, : 3 * C1]
    proj[...] = joined[:, 3 * C1 :]
    up[...] = take(packed, 1152, C1, 6) * factor
    down[...] = take(packed, 2304, C1, 6) * factor


def assemble_kernel(ids, own, own_two, lon, lat, corner, place, place_two, tokens, two):
    high, low = halves(jnp.concatenate([lon[...], lat[...], corner[...]], axis=0))
    cells = own[...] + (nn(place[...], high) + nn(place[...], low))
    for row in range(12):
        tokens[row] = cells[row * 24 : (row + 1) * 24]
    cells = own_two[...] + (nn(place_two[...], high) + nn(place_two[...], low))
    for row in range(6):
        for level in range(2):
            at = level * 72 + row * 12
            two[row, :, level * C2 : (level + 1) * C2] = cells[at : at + 12]


def per_device(
    tokens, cotangent, bias_one, qkv_one, proj_one, up_one, down_one,
    merge_weight, bias_two, qkv_two, proj_two, up_two, down_two,
):
    lon = ("chip", "core")
    both = ("lat", "chip", "core")
    lats, lons = lax.axis_size("lat"), lax.axis_size(lon)
    ids = jnp.stack([lax.axis_index(name) for name in both]).astype(jnp.int32)
    factor = (WINDOW * lats * lons) ** -0.5
    from_right = [((i + 1) % lons, i) for i in range(lons)]
    to_right = [(i, (i + 1) % lons) for i in range(lons)]
    from_up = [(i, (i + 1) % lats) for i in range(lats)]
    to_up = [((i + 1) % lats, i) for i in range(lats)]
    down_one = down_one.T
    corner_in = [
        (i * lons + (j + 1) % lons, (i + 1) % lats * lons + j) for i in range(lats) for j in range(lons)
    ]
    corner_out = [
        ((i + 1) % lats * lons + j, i * lons + (j + 1) % lons) for i in range(lats) for j in range(lons)
    ]
    for_left, for_down = pack(tokens[0], cotangent[0])
    right = lax.ppermute(for_left, lon, from_right)
    up = lax.ppermute(for_down, "lat", from_up)
    diag = lax.ppermute(for_down, both, corner_in)

    bias_a, bias_b, bias_c = expand_bias(ids, bias_one, bias_two, *bias_constants())
    select, gather, cot_select, strips, back_own, back_strips = constants()
    mask, mask_t, fold = blocks_of_heads()
    out_two, xw, grad_own, lon_strip, lat_strip, corner, mine_two, theirs_two = upper(
        ids, tokens[0], cotangent[0], right, up, diag, bias_a, bias_b, bias_c,
        qkv_one, proj_one, up_one, down_one, merge_weight, qkv_two, proj_two, up_two, down_two,
        select, gather, cot_select, strips, mask, mask_t, fold,
    )
    lon_strip = lax.ppermute(lon_strip, lon, to_right)
    lat_strip = lax.ppermute(lat_strip, "lat", to_up)
    corner = lax.ppermute(corner, both, corner_out)
    other_core = [(i, 1 - i) for i in range(2)]
    theirs_two = lax.ppermute(theirs_two, "core", other_core)
    result = lambda *dims: jax.ShapeDtypeStruct(dims, F32)
    blocks = lambda rows: jax.ShapeDtypeStruct((CHIPS, rows, LANES), BF16)
    chips = ("lat", "chip")
    packed_two = call(chip_kernel, "chip_two", 3, 16, blocks(UPPER_BLOCK), (ids, mine_two, theirs_two))
    packed_two, lon_strip, lat_strip, corner = lax.optimization_barrier(
        (packed_two, lon_strip, lat_strip, corner)
    )
    packed_two = lax.all_to_all(packed_two, chips, 0, 0, tiled=True)

    to_tokens, to_two, place, place_two = output_constants()
    own_cells, own_two, lon_strip, lat_strip, corner, mine_one, theirs_one = lower(
        ids, xw, out_two, grad_own, lon_strip, lat_strip, corner, bias_a, bias_b,
        qkv_one, proj_one, up_one, down_one,
        back_own, back_strips, to_tokens, to_two, mask, mask_t, fold,
    )
    theirs_one = lax.ppermute(theirs_one, "core", other_core)
    packed_one = call(chip_kernel, "chip_one", 1, 16, blocks(LOWER_BLOCK), (ids, mine_one, theirs_one))
    packed_two, packed_one = lax.optimization_barrier((packed_two, packed_one))
    merged = call(
        middle_kernel, "middle", 2, 16, blocks(UPPER_BLOCK + LOWER_BLOCK), (ids, packed_two, packed_one)
    )
    merged = lax.all_to_all(merged, chips, 0, 0, tiled=True)
    summed_one = call(total_kernel, "total_one", 1, 16, blocks(LOWER_BLOCK), (ids, merged))
    gathered_one = lax.all_to_all(summed_one, chips, 0, 0, tiled=True)

    sums_two = call(
        functools.partial(upper_last_kernel, factor), "last_two", 5, 32,
        tuple(result(*w.shape) for w in (merge_weight, qkv_two, proj_two, up_two, down_two)),
        (ids, merged, lax.ppermute(merged, "core", other_core)),
        [pltpu.VMEM((2, CHIPS * UPPER_BLOCK, LANES), BF16)],
    )
    lon_strip = lax.ppermute(lon_strip, lon, to_right)
    lat_strip = lax.ppermute(lat_strip, "lat", to_up)
    corner = lax.ppermute(corner, both, corner_out)
    grad_tokens, out_two = call(
        assemble_kernel, "assemble", 3, 8, (result(12, 24, 2 * C1), result(6, 12, 2 * C2)),
        (ids, own_cells, own_two, lon_strip, lat_strip, corner, place, place_two),
    )
    gathered_one, grad_tokens, out_two, *sums_two = lax.optimization_barrier(
        (gathered_one, grad_tokens, out_two, *sums_two)
    )
    sums_one = call(
        functools.partial(lower_last_kernel, factor), "last_one", 2, 32,
        tuple(result(*w.shape) for w in (qkv_one, proj_one, up_one, down_one)),
        (ids, gathered_one, lax.ppermute(gathered_one, "core", other_core)),
        [pltpu.VMEM((2, CHIPS * LOWER_BLOCK, LANES), BF16)],
    )
    return (out_two[None], grad_tokens[None], *sums_one[:3], sums_one[3].T, *sums_two)


def solution(mesh):
    lats, lons = mesh.devices.shape
    mesh = Mesh(mesh.devices.reshape(lats, lons // 2, 2), ("lat", "chip", "core"))
    sharded, copied = P(None, "lat", ("chip", "core"), None), P()
    return jax.shard_map(
        per_device,
        mesh=mesh,
        in_specs=(sharded, sharded) + (copied,) * 11,
        out_specs=(sharded, sharded) + (copied,) * 9,
        check_vma=False,
    )
```

```python
import functools

import jax
import jax.numpy as jnp
import numpy as np
from jax import lax
from jax.experimental import pallas as pl
from jax.experimental.pallas import tpu as pltpu
from jax.sharding import Mesh, PartitionSpec as P

C1 = 192
C2 = 384
HEAD = 32
LEVELS = 2
WLAT = 6
WLON = 12
WINDOW = 144
REL = 2 * WLON - 1
COLUMN = LEVELS * WLAT
FACTOR = HEAD**-0.5
EPSILON = 1e-05
MASKED = -1e30
GROUPS_ONE = ((0, 4), (4, 2))
GROUPS_TWO = ((0, 4), (4, 4), (8, 4))
STRIPS = (112, 112, 48)
MIB = 1024 * 1024
SHIFT = (96, 96, 64)
SHIFT_TOKENS = (56, 56, 24)
LANES = 128
CHIPS = 64
UPPER_BLOCK = 128
LOWER_BLOCK = 32
F32 = jnp.float32
BF16 = jnp.bfloat16


def constants():
    select = np.zeros((2, 432, 288), np.float32)
    for col in range(36):
        half, source = (0, 6 + col) if col < 18 else (1, col - 18)
        for level in range(2):
            for a in range(6):
                select[level, col * 12 + level * 6 + a, half * 144 + a * 24 + source] = 1
    own = {}
    gather = np.zeros((3, 576, 432), np.float32)
    for pr in range(2):
        for pc in range(2):
            for out_col in range(12):
                for level in range(2):
                    for out_row in range(6):
                        row, col = 3 + 2 * out_row + pr, 6 + 2 * out_col + pc
                        place = (pr * 2 + pc) * 144 + out_col * 12 + level * 6 + out_row
                        gather[row // 6, place, col * 12 + level * 6 + row % 6] = 1
                        own[row, col, level] = place
    cot_select = np.zeros((144, 288), np.float32)
    for out_col in range(12):
        for out_row in range(6):
            for level in range(2):
                up, right = out_row < 3, out_col >= 6
                block = (2 if up else 0) + (1 if right else 0)
                col = out_col - 6 if right else 6 + out_col
                place = out_col * 12 + level * 6 + out_row
                cot_select[place, block * 72 + out_row % 3 * 24 + level * 12 + col] = 1
    strips = np.zeros((sum(STRIPS), 576), np.float32)
    back_own = np.zeros((576, 576), np.float32)
    back_strips = np.zeros((576, sum(STRIPS)), np.float32)
    for row in range(6, 18):
        for col in range(24):
            for level in range(2):
                target = (row - 6) // 6 * 288 + col * 12 + level * 6 + row % 6
                if row <= 14 and col >= 6:
                    back_own[target, own[row, col, level]] = 1
                    continue
                if row <= 14:
                    place = (row - 6) * 12 + col * 2 + level
                    sent = (row, 24 + col, level)
                elif col >= 6:
                    place = STRIPS[0] + (row - 15) * 36 + (col - 6) * 2 + level
                    sent = (row - 12, col, level)
                else:
                    place = STRIPS[0] + STRIPS[1] + (row - 15) * 12 + col * 2 + level
                    sent = (row - 12, 24 + col, level)
                back_strips[target, place] = 1
                strips[place, own[sent]] = 1
    return tuple(jnp.asarray(v, BF16) for v in (select, gather, cot_select, strips, back_own, back_strips))


def output_constants():
    starts = (0, SHIFT[0], SHIFT[0] + SHIFT[1])
    tokens = np.zeros((2, 288 + sum(SHIFT_TOKENS), 576), np.float32)
    place = np.zeros((288, sum(SHIFT)), np.float32)
    two = np.zeros((144 + sum(SHIFT) - sum(SHIFT_TOKENS), WINDOW), np.float32)
    place_two = np.zeros((144, sum(SHIFT)), np.float32)

    def strip(row, col, rows, cols):
        if row < rows:
            return (None, row, col - cols) if col >= cols else (0, row, col)
        return (1, row - rows, col - cols) if col >= cols else (2, row - rows, col)

    for row in range(12):
        for col in range(24):
            kind, sub_row, sub_col = strip(row, col, 9, 6)
            source_row = row + 3 if row < 9 else row - 9
            source_col = col - 6 if col >= 6 else col + 18
            if kind is None:
                target = row * 24 + col
            else:
                at = sub_row * (18 if kind == 1 else 6) + sub_col
                target = 288 + sum(SHIFT_TOKENS[:kind]) + at
                place[row * 24 + col, starts[kind] + at] = 1
            for level in range(2):
                source = source_row // 6 * 288 + source_col * 12 + level * 6 + source_row % 6
                tokens[level, target, source] = 1
    for row in range(6):
        for col in range(12):
            kind, sub_row, sub_col = strip(row, col, 3, 6)
            source_row = row + 3 if row < 3 else row - 3
            source_col = col - 6 if col >= 6 else col + 6
            for level in range(2):
                if kind is None:
                    target = level * 72 + row * 12 + col
                else:
                    at = level * 18 + sub_row * 6 + sub_col
                    target = 144 + kind * 40 + at
                    place_two[level * 72 + row * 12 + col, starts[kind] + SHIFT_TOKENS[kind] + at] = 1
                two[target, source_col * 12 + level * 6 + source_row] = 1
    return tuple(jnp.asarray(v, BF16) for v in (tokens, two, place, place_two))


def bias_constants():
    z1, z2, a1, a2, r = (v.reshape(-1) for v in np.indices((LEVELS, LEVELS, WLAT, WLAT, REL)))
    half = WLAT // 2
    kind = np.where((a1 < half) & (a2 < half), 0, np.where((a1 >= half) & (a2 >= half), 1, 2))
    codes = np.stack([kind, z2, a2 + 2 * (1 - z2), r * COLUMN + z1 * WLAT + a1])
    return jnp.asarray(codes, F32)


def blocks_of_heads():
    mask = (np.arange(576)[:, None] // WINDOW == np.arange(128)[None] // HEAD).astype(np.float32)
    fold = (np.arange(WINDOW)[:, None] == np.arange(576)[None] % WINDOW).astype(np.float32)
    return tuple(jnp.asarray(v, BF16) for v in (mask, mask.T, fold))


def params(microseconds, vmem):
    return {
        "compiler_params": pltpu.CompilerParams(vmem_limit_bytes=vmem * MIB),
        "cost_estimate": pl.CostEstimate(
            flops=int(microseconds * 1e9), bytes_accessed=int(microseconds * 3e6), transcendentals=0
        ),
    }


def nn(left, right):
    return jnp.dot(left, right, preferred_element_type=F32)


def nt(left, right):
    return lax.dot_general(left, right, (((1,), (1,)), ((), ())), preferred_element_type=F32)


def tn(left, right):
    return lax.dot_general(left, right, (((0,), (0,)), ((), ())), preferred_element_type=F32)


def layer_norm(values):
    average = jnp.mean(values, axis=-1, keepdims=True)
    centred = values - average
    scale = lax.rsqrt(jnp.mean(centred * centred, axis=-1, keepdims=True) + EPSILON)
    return centred * scale, scale


def layer_norm_back(grad, normed, scale):
    first = jnp.mean(grad, axis=-1, keepdims=True)
    second = jnp.mean(grad * normed, axis=-1, keepdims=True)
    return scale * (grad - first - normed * second)


GELU_A = (2.0 / np.pi) ** 0.5
GELU_B = 0.044715


def gelu(values):
    tanh = jnp.tanh(GELU_A * (values + GELU_B * (values * values * values)))
    return 0.5 * values * (1.0 + tanh)


def gelu_both(values):
    square = values * values
    tanh = jnp.tanh(GELU_A * values * (1.0 + GELU_B * square))
    half = 0.5 * (1.0 + tanh)
    slope = half + 0.5 * values * (1.0 - tanh * tanh) * (GELU_A * (1.0 + 3.0 * GELU_B * square))
    return values * half, slope


def spread(values, mask, heads):
    return jnp.concatenate([values] * heads, axis=0) * mask[: heads * WINDOW, : heads * HEAD]


def pull(left, right, mask_t, fold, heads):
    both = tn(left, right).astype(BF16) * mask_t[: heads * HEAD, : heads * WINDOW]
    return nt(fold[:, : heads * WINDOW], both)


def attend(parts, mask, mask_t, fold):
    scores = [
        nt(keys, spread(queries, mask, heads)) * FACTOR + bias for queries, keys, _, bias, heads in parts
    ]
    powers = [jnp.exp(score - jnp.max(score, axis=0, keepdims=True)) for score in scores]
    chances = [power * (1.0 / jnp.sum(power, axis=0, keepdims=True)) for power in powers]
    taken = [
        pull(part[2], chance.astype(BF16), mask_t, fold, part[4]) for part, chance in zip(parts, chances)
    ]
    return taken, chances


def attend_back(parts, mask, mask_t, fold):
    grads = [spread(part[4], mask, part[5]) for part in parts]
    grad_chances = [nt(part[2], grad) for part, grad in zip(parts, grads)]
    grad_values = [nn(part[3].astype(BF16), grad) for part, grad in zip(parts, grads)]
    products = [grad * part[3] for part, grad in zip(parts, grad_chances)]
    grad_scores = [
        ((product - part[3] * jnp.sum(product, axis=0, keepdims=True)) * FACTOR).astype(BF16)
        for part, product in zip(parts, products)
    ]
    grad_keys = [nn(grad, spread(part[0], mask, part[5])) for part, grad in zip(parts, grad_scores)]
    grad_queries = [
        pull(part[1], grad, mask_t, fold, part[5]) for part, grad in zip(parts, grad_scores)
    ]
    return grad_queries, grad_keys, grad_values


SPANS = (((0, 896), (1536, 2560)), ((768, 1664), (2432, 3312)))


def bias_kernel(ids, one, two, codes, first_ref, second_ref, two_out_ref, pieces, table):
    band = ids[0]
    kind, level_of, row_of, place_of = (codes[i : i + 1, :] for i in range(4))
    places = lax.broadcasted_iota(jnp.int32, (REL * COLUMN, codes.shape[1]), 0).astype(F32)
    lanes = jnp.where(places == place_of, 1.0, 0.0).astype(BF16)
    row = lax.broadcasted_iota(jnp.int32, (8, codes.shape[1]), 0).astype(F32)

    def window(source, index):
        count = source.shape[0] - 1
        index = lax.rem(index + count, count)
        mixed = jnp.where(
            kind == 0.0, source[count], jnp.where(kind == 1.0, source[0], MASKED)
        )
        return jnp.where(index == 0, mixed, source[index])

    values = [
        window(one, 2 * band - 1), window(one, 2 * band), window(one, 2 * band + 1), window(two, band)
    ]
    heads = sum(value.shape[0] for value in values)
    for level in range(2):
        slot = 0
        rows = (row == row_of) & (level_of == float(level))
        for value in values:
            high = value.astype(BF16).astype(F32)
            low = value - high
            for h in range(0, value.shape[0], 2):
                for piece, taken in enumerate((high, low)):
                    at = 0
                    for start, stop in SPANS[level]:
                        chosen = rows[:, start:stop]
                        pair = [
                            jnp.where(chosen, taken[h + i : h + i + 1, start:stop], 0.0) for i in range(2)
                        ]
                        pieces[piece, (slot + h) * 8 : (slot + h) * 8 + 16, at : at + stop - start] = (
                            jnp.concatenate(pair, axis=0).astype(BF16)
                        )
                        at += stop - start
            slot += value.shape[0]
        total = None
        for piece in range(2):
            at = 0
            for start, stop in SPANS[level]:
                term = nt(pieces[piece, :, at : at + stop - start], lanes[:, start:stop])
                total = term if total is None else total + term
                at += stop - start
        for h in range(heads):
            table[h, level * 8 : level * 8 + 8, :] = total[h * 8 : h * 8 + 8]

    for base, count, groups, targets in (
        (0, 3, GROUPS_ONE, (first_ref, second_ref)),
        (18, 1, GROUPS_TWO, (two_out_ref, two_out_ref, two_out_ref)),
    ):
        for row in range(count):
            for index, (start, heads) in enumerate(groups):
                target = targets[index]
                place = row if count == 3 else index
                which = [base + row * 6 + start + h for h in range(heads)]
                for o2 in range(WLON):
                    left = (WLON - 1 - o2) * COLUMN
                    piece = [table[h, 2 : 2 + COLUMN, left : left + WINDOW] for h in which]
                    target[place, o2 * COLUMN : (o2 + 1) * COLUMN, :] = jnp.concatenate(piece, axis=1)


def expand_bias(*operands):
    return pl.pallas_call(
        bias_kernel,
        in_specs=specs(len(operands)),
        out_shape=(
            jax.ShapeDtypeStruct((3, WINDOW, 576), F32),
            jax.ShapeDtypeStruct((3, WINDOW, 288), F32),
            jax.ShapeDtypeStruct((3, WINDOW, 576), F32),
        ),
        scratch_shapes=[
            pltpu.VMEM((2, 240, 1920), BF16),
            pltpu.VMEM((30, 16, REL * COLUMN), F32),
        ],
        **params(7, 24),
        name="bias_expand",
    )(*operands)


def pack_kernel(tokens, cot, right_ref, up_ref):
    for out, row, cot_row in ((right_ref, 0, 0), (up_ref, 3, 3)):
        out[:9] = tokens[row : row + 9]
        for r in range(3):
            value = cot[cot_row + r].astype(F32)
            out[9 + r] = jnp.concatenate([value[:, :C2], value[:, C2:]], axis=0).astype(BF16)


def pack(tokens, cot):
    shape = jax.ShapeDtypeStruct((12, 24, 2 * C1), BF16)
    return pl.pallas_call(
        pack_kernel, out_shape=(shape, shape), name="pack", **params(2, 8)
    )(tokens, cot)


def put(packed, base, value):
    half, count = packed.shape[1], value.shape[0]
    for j in range(value.shape[1] // LANES):
        start, stop = base + j * count, base + (j + 1) * count
        lanes = value[:, j * LANES : (j + 1) * LANES]
        for part in range(2):
            low, high = max(start, part * half), min(stop, (part + 1) * half)
            if low < high:
                packed[part, low - part * half : high - part * half, :] = lanes[low - start : high - start]
    return base + value.shape[0] * value.shape[1] // LANES


def take(packed, base, count, columns):
    half, lanes = packed.shape[1], []
    for j in range(columns):
        start, stop, rows = base + j * count, base + (j + 1) * count, []
        for part in range(2):
            low, high = max(start, part * half), min(stop, (part + 1) * half)
            if low < high:
                rows.append(packed[part, low - part * half : high - part * half, :])
        lanes.append(rows[0] if len(rows) == 1 else jnp.concatenate(rows, axis=0))
    return jnp.concatenate(lanes, axis=1).astype(F32)


def send_half(ids, packed, half, mine_ref, theirs_ref, sems, start):
    for target, own in ((mine_ref, half), (theirs_ref, 1 - half)):

        @pl.when(ids[2] == own)
        def _():
            copy = pltpu.make_async_copy(packed.at[half], target, sems.at[half])
            if start:
                copy.start()
            else:
                copy.wait()


def upper_kernel(
    ids, own, cot_own, right, up, diag,
    bias_a, bias_b, bias_two,
    qkv_one, proj_one, up_one, down_one, merge, qkv_two, proj_two, up_two, down_two,
    select, gather, cot_select, strips, mask_ref, mask_t_ref, fold_ref,
    out_ref, xw_ref, grad_ref, lon_ref, lat_ref, corner_ref, mine_ref, theirs_ref,
    q_ref, k_ref, v_ref, att_ref, xm_ref, am_ref, one_ref, p_ref, packed, sems,
):
    mask, mask_t, fold = mask_ref[...], mask_t_ref[...], fold_ref[...]

    def rows_of(block, start, count):
        return [block[start + r].astype(F32) for r in range(count)]

    for wr in range(3):
        if wr == 0:
            left, other = rows_of(up, 0, 6), rows_of(diag, 0, 6)
        elif wr == 1:
            left = rows_of(up, 6, 3) + rows_of(own, 0, 3)
            other = rows_of(diag, 6, 3) + rows_of(right, 0, 3)
        else:
            left, other = rows_of(own, 3, 6), rows_of(right, 3, 6)
        source = jnp.concatenate(left + other, axis=0).astype(BF16)
        cells = nn(select[0], source[:, :C1]) + nn(select[1], source[:, C1:])
        xw_ref[wr] = cells.astype(BF16)
        normed = layer_norm(cells)[0].astype(BF16)
        projected = nn(normed, qkv_one[...]).astype(BF16)
        q_ref[wr] = projected[:, :C1]
        k_ref[wr] = projected[:, C1 : 2 * C1]
        v_ref[wr] = projected[:, 2 * C1 :]

    @pl.loop(0, 3)
    def _(wr):
        places = [
            (slice(wc * WINDOW, (wc + 1) * WINDOW), slice(start * HEAD, (start + heads) * HEAD), heads)
            for wc in range(3)
            for start, heads in GROUPS_ONE
        ]
        parts = [
            (
                q_ref[wr, rows, lanes], k_ref[wr, rows, lanes], v_ref[wr, rows, lanes],
                bias_a[wr] if heads == 4 else bias_b[wr], heads,
            )
            for rows, lanes, heads in places
        ]
        taken, _ = attend(parts, mask, mask_t, fold)
        for (rows, lanes, heads), value in zip(places, taken):
            att_ref[wr, rows, lanes] = value.astype(BF16)

    xm_ref[...] = nn(gather[0], xw_ref[0]) + nn(gather[1], xw_ref[1]) + nn(gather[2], xw_ref[2])
    am_ref[...] = (
        nn(gather[0], att_ref[0]) + nn(gather[1], att_ref[1]) + nn(gather[2], att_ref[2])
    ).astype(BF16)

    for half in range(2):
        rows = slice(half * 288, (half + 1) * 288)
        middle = xm_ref[rows, :] + nn(am_ref[rows, :], proj_one[...])
        normed = layer_norm(middle)[0].astype(BF16)
        active = gelu(nn(normed, up_one[...])).astype(BF16)
        one_ref[rows, :] = middle + nt(active, down_one[...])

    parts = [one_ref[g * WINDOW : (g + 1) * WINDOW, :] for g in range(4)]
    average = sum(jnp.sum(part, axis=-1, keepdims=True) for part in parts) / (4 * C1)
    spread_of = sum(
        jnp.sum((part - average) * (part - average), axis=-1, keepdims=True) for part in parts
    ) / (4 * C1)
    merge_scale = lax.rsqrt(spread_of + EPSILON)
    merged = [((part - average) * merge_scale) for part in parts]
    merged_low = [part.astype(BF16) for part in merged]
    grid = sum(nn(merged_low[g], merge[g * C1 : (g + 1) * C1, :]) for g in range(4))

    normed_full, scale = layer_norm(grid)
    normed = normed_full.astype(BF16)
    q, k, v = (nn(normed, qkv_two[:, j * C2 : (j + 1) * C2]).astype(BF16) for j in range(3))
    lanes_of = [slice(start * HEAD, (start + heads) * HEAD) for start, heads in GROUPS_TWO]
    taken, chances = attend(
        [(q[:, at], k[:, at], v[:, at], bias_two[index], 4) for index, at in enumerate(lanes_of)],
        mask, mask_t, fold,
    )
    for index in range(3):
        p_ref[index] = chances[index]
    attended = jnp.concatenate([value.astype(BF16) for value in taken], axis=1)
    middle = grid + nn(attended, proj_two[...])
    normed_two_full, scale_two = layer_norm(middle)
    normed_two = normed_two_full.astype(BF16)
    active, slope = gelu_both(nn(normed_two, up_two[...]))
    active = active.astype(BF16)
    out_ref[...] = middle + nn(active, down_two[...])

    cot = []
    for r in range(3):
        value = cot_own[r].astype(F32)
        cot += [value[:, :C2], value[:, C2:]]
    for block in (right, up, diag):
        cot += rows_of(block, 9, 3)
    grad = nn(cot_select[...], jnp.concatenate(cot, axis=0).astype(BF16))
    grad_low = grad.astype(BF16)
    put(packed, 4608, tn(active, grad_low).astype(BF16))
    grad_raised = (nt(grad_low, down_two[...]) * slope).astype(BF16)
    put(packed, 0, tn(normed_two, grad_raised).astype(BF16))
    send_half(ids, packed, 0, mine_ref, theirs_ref, sems, True)
    grad_middle = grad + layer_norm_back(nt(grad_raised, up_two[...]), normed_two_full, scale_two)
    grad_middle_low = grad_middle.astype(BF16)
    put(packed, 9216, tn(attended, grad_middle_low).astype(BF16))
    grad_attended = nt(grad_middle_low, proj_two[...]).astype(BF16)
    pieces = attend_back(
        [
            (q[:, at], k[:, at], v[:, at], p_ref[index], grad_attended[:, at], 4)
            for index, at in enumerate(lanes_of)
        ],
        mask, mask_t, fold,
    )
    grad_normed = None
    for j in range(3):
        part = jnp.concatenate([value.astype(BF16) for value in pieces[j]], axis=1)
        put(packed, 10368 + j * 1152, tn(normed, part).astype(BF16))
        term = nt(part, qkv_two[:, j * C2 : (j + 1) * C2])
        grad_normed = term if grad_normed is None else grad_normed + term
    grad_grid = (grad_middle + layer_norm_back(grad_normed, normed_full, scale)).astype(BF16)

    grad_parts = []
    grad_merge = [tn(merged_low[g], grad_grid).astype(BF16) for g in range(4)]
    put(packed, 13824, jnp.concatenate(grad_merge, axis=0))
    packed[1, 16128 - packed.shape[1] :, :] = jnp.zeros((256, LANES), BF16)
    send_half(ids, packed, 1, mine_ref, theirs_ref, sems, True)
    for g in range(4):
        grad_parts.append(nt(grad_grid, merge[g * C1 : (g + 1) * C1, :]))
    first = sum(jnp.sum(part, axis=-1, keepdims=True) for part in grad_parts) / (4 * C1)
    second = sum(
        jnp.sum(part * kept, axis=-1, keepdims=True) for part, kept in zip(grad_parts, merged)
    ) / (4 * C1)
    for g in range(4):
        grad_ref[g * WINDOW : (g + 1) * WINDOW, :] = (
            merge_scale * (grad_parts[g] - first - merged[g] * second)
        ).astype(BF16)
    sent = nn(strips[...], grad_ref[...]).astype(BF16)
    lon_ref[...] = sent[: STRIPS[0]]
    lat_ref[...] = sent[STRIPS[0] : STRIPS[0] + STRIPS[1]]
    corner_ref[...] = sent[STRIPS[0] + STRIPS[1] :]
    for half in range(2):
        send_half(ids, packed, half, mine_ref, theirs_ref, sems, False)


def packed_shape(block):
    return jax.ShapeDtypeStruct((CHIPS * block, LANES), BF16)


def specs(count):
    vmem = pl.BlockSpec(memory_space=pltpu.VMEM)
    return [pl.BlockSpec(memory_space=pltpu.SMEM)] + [vmem] * (count - 1)


def out_specs(count, last_any):
    vmem, left = pl.BlockSpec(memory_space=pltpu.VMEM), pl.BlockSpec(memory_space=pl.ANY)
    return tuple([vmem] * (count - last_any) + [left] * last_any)


def upper(*operands):
    shape = jax.ShapeDtypeStruct
    return pl.pallas_call(
        upper_kernel,
        in_specs=specs(len(operands)),
        out_specs=out_specs(8, 2),
        out_shape=(
            shape((WINDOW, C2), F32),
            shape((3, 432, C1), BF16),
            shape((576, C1), BF16),
            shape((STRIPS[0], C1), BF16),
            shape((STRIPS[1], C1), BF16),
            shape((STRIPS[2], C1), BF16),
            packed_shape(UPPER_BLOCK),
            packed_shape(UPPER_BLOCK),
        ),
        scratch_shapes=[
            pltpu.VMEM((3, 432, C1), BF16),
            pltpu.VMEM((3, 432, C1), BF16),
            pltpu.VMEM((3, 432, C1), BF16),
            pltpu.VMEM((3, 432, C1), BF16),
            pltpu.VMEM((576, C1), F32),
            pltpu.VMEM((576, C1), BF16),
            pltpu.VMEM((576, C1), F32),
            pltpu.VMEM((3, WINDOW, 576), F32),
            pltpu.VMEM((2, CHIPS * UPPER_BLOCK, LANES), BF16),
            pltpu.SemaphoreType.DMA((2,)),
        ],
        **params(25, 40),
        name="upper",
    )(*operands)


def window_places(row, pa_ref, pb_ref):
    return [
        (
            pl.ds(pl.multiple_of(row * 288 + wc * WINDOW, WINDOW), WINDOW),
            slice(start * HEAD, (start + heads) * HEAD),
            heads,
            (pa_ref if heads == 4 else pb_ref, row * 2 + wc),
        )
        for wc in range(2)
        for start, heads in GROUPS_ONE
    ]


def halves(value):
    high = value.astype(BF16)
    return high, (value - high.astype(F32)).astype(BF16)


def lower_forward_kernel(
    xw, bias_a, bias_b, qkv_one, proj_one, up_one, mask_ref, mask_t_ref, fold_ref,
    normed_ref, full_ref, scale_ref, q_ref, k_ref, v_ref, pa_ref, pb_ref, att_ref,
    normed_two_ref, full_two_ref, scale_two_ref, act_ref, slope_ref,
):
    mask, mask_t, fold = mask_ref[...], mask_t_ref[...], fold_ref[...]
    row_slices = [slice(row * 288, (row + 1) * 288) for row in range(2)]
    for row, rows in enumerate(row_slices):
        full, scale = layer_norm(xw[1 + row, :288, :].astype(F32))
        full_ref[rows, :] = full
        scale_ref[rows, :] = scale
        normed = full.astype(BF16)
        normed_ref[rows, :] = normed
        projected = nn(normed, qkv_one[...]).astype(BF16)
        q_ref[rows, :] = projected[:, :C1]
        k_ref[rows, :] = projected[:, C1 : 2 * C1]
        v_ref[rows, :] = projected[:, 2 * C1 :]

    @pl.loop(0, 2)
    def _(row):
        places = window_places(row, pa_ref, pb_ref)
        parts = [
            (
                q_ref[rows, at], k_ref[rows, at], v_ref[rows, at],
                bias_a[1 + row] if heads == 4 else bias_b[1 + row], heads,
            )
            for rows, at, heads, _ in places
        ]
        taken, chances = attend(parts, mask, mask_t, fold)
        for (rows, at, _, (kept, window)), value, chance in zip(places, taken, chances):
            att_ref[rows, at] = value.astype(BF16)
            kept[window] = chance

    for row, rows in enumerate(row_slices):
        middle = xw[1 + row, :288, :].astype(F32) + nn(att_ref[rows, :], proj_one[...])
        full, scale = layer_norm(middle)
        full_two_ref[rows, :] = full
        scale_two_ref[rows, :] = scale
        normed_two = full.astype(BF16)
        normed_two_ref[rows, :] = normed_two
        active, slope = gelu_both(nn(normed_two, up_one[...]))
        act_ref[rows, :] = active.astype(BF16)
        slope_ref[rows, :] = slope


def lower_forward(*operands):
    shape = jax.ShapeDtypeStruct
    wide, full, scale = shape((576, C1), BF16), shape((576, C1), F32), shape((576, 1), F32)
    return pl.pallas_call(
        lower_forward_kernel,
        out_shape=(
            wide, full, scale, wide, wide, wide,
            shape((4, WINDOW, 576), F32), shape((4, WINDOW, 288), F32), wide,
            wide, full, scale, shape((576, 768), BF16), shape((576, 768), F32),
        ),
        name="lower_forward",
        **params(5, 32),
    )(*operands)


def lower_kernel(
    ids, out_two, own, lon, lat, corner,
    normed_ref, full_ref, scale_ref, q_ref, k_ref, v_ref, pa_ref, pb_ref, att_ref,
    normed_two_ref, full_two_ref, scale_two_ref, act_ref, slope_ref,
    qkv_one, proj_one, up_one, down_one,
    back_own, back_strips, to_tokens, to_two, mask_ref, mask_t_ref, fold_ref,
    out_ref, out_two_ref, lon_ref, lat_ref, corner_ref, mine_ref, theirs_ref,
    gs_ref, raised_ref, gm_ref, gml_ref, ga_ref, gq_ref, gk_ref, gv_ref, gx_ref,
    packed, sems,
):
    mask, mask_t, fold = mask_ref[...], mask_t_ref[...], fold_ref[...]
    arrived = jnp.concatenate([lon[...], lat[...], corner[...]], axis=0)
    gs_ref[...] = nn(back_own[...], own[...]) + nn(back_strips[...], arrived)
    row_slices = [slice(row * 288, (row + 1) * 288) for row in range(2)]

    for rows in row_slices:
        grad = gs_ref[rows, :]
        grad_raised = (nn(grad.astype(BF16), down_one[...]) * slope_ref[rows, :]).astype(BF16)
        raised_ref[rows, :] = grad_raised
        grad_middle = grad + layer_norm_back(
            nt(grad_raised, up_one[...]), full_two_ref[rows, :], scale_two_ref[rows, :]
        )
        gm_ref[rows, :] = grad_middle
        low = grad_middle.astype(BF16)
        gml_ref[rows, :] = low
        ga_ref[rows, :] = nt(low, proj_one[...]).astype(BF16)

    @pl.loop(0, 2)
    def _(row):
        places = window_places(row, pa_ref, pb_ref)
        parts = [
            (q_ref[rows, at], k_ref[rows, at], v_ref[rows, at], kept[window], ga_ref[rows, at], heads)
            for rows, at, heads, (kept, window) in places
        ]
        grads = attend_back(parts, mask, mask_t, fold)
        for target, values in zip((gq_ref, gk_ref, gv_ref), grads):
            for (rows, at, _, _), value in zip(places, values):
                target[rows, at] = value.astype(BF16)

    normed = normed_ref[...]
    grads = [tn(normed, ref[...]) for ref in (gq_ref, gk_ref, gv_ref)]
    grads = jnp.concatenate(grads + [tn(att_ref[...], gml_ref[...])], axis=1)
    put(packed, 0, grads.astype(BF16))
    put(packed, 1152, tn(normed_two_ref[...], raised_ref[...]).astype(BF16))
    put(packed, 2304, tn(gs_ref[...].astype(BF16), act_ref[...]).astype(BF16))
    packed[1, 3456 - packed.shape[1] :, :] = jnp.zeros((640, LANES), BF16)
    for half in range(2):
        send_half(ids, packed, half, mine_ref, theirs_ref, sems, True)

    for rows in row_slices:
        grad_normed = (
            nt(gq_ref[rows, :], qkv_one[:, :C1])
            + nt(gk_ref[rows, :], qkv_one[:, C1 : 2 * C1])
            + nt(gv_ref[rows, :], qkv_one[:, 2 * C1 :])
        )
        gx_ref[rows, :] = gm_ref[rows, :] + layer_norm_back(
            grad_normed, full_ref[rows, :], scale_ref[rows, :]
        )
    high, low = halves(gx_ref[...])
    cells = jnp.concatenate(
        [nn(to_tokens[level], high) + nn(to_tokens[level], low) for level in range(2)], axis=1
    )
    high, low = halves(out_two[...])
    two = nn(to_two[...], high) + nn(to_two[...], low)
    out_ref[...] = cells[:288]
    out_two_ref[...] = two[:144]
    at = 288
    for kind, ref in enumerate((lon_ref, lat_ref, corner_ref)):
        count = SHIFT_TOKENS[kind]
        strip = [cells[at : at + count], two[144 + kind * 40 : 144 + (kind + 1) * 40]]
        ref[...] = jnp.concatenate(strip, axis=0).astype(BF16)
        at += count
    for half in range(2):
        send_half(ids, packed, half, mine_ref, theirs_ref, sems, False)


def lower(*operands):
    shape = jax.ShapeDtypeStruct
    wide = pltpu.VMEM((576, C1), BF16)
    return pl.pallas_call(
        lower_kernel,
        in_specs=specs(len(operands)),
        out_specs=out_specs(7, 2),
        out_shape=(
            shape((288, C2), F32),
            shape((144, C2), F32),
            *(shape((count, C2), BF16) for count in SHIFT),
            packed_shape(LOWER_BLOCK),
            packed_shape(LOWER_BLOCK),
        ),
        scratch_shapes=[
            pltpu.VMEM((576, C1), F32),
            pltpu.VMEM((576, 768), BF16),
            pltpu.VMEM((576, C1), F32),
            wide, wide, wide, wide, wide,
            pltpu.VMEM((576, C1), F32),
            pltpu.VMEM((2, CHIPS * LOWER_BLOCK, LANES), BF16),
            pltpu.SemaphoreType.DMA((2,)),
        ],
        **params(10, 32),
        name="lower",
    )(*operands)


def call(kernel, name, microseconds, vmem, out_shape, operands, scratch=()):
    return pl.pallas_call(
        kernel,
        in_specs=specs(len(operands)),
        out_shape=out_shape,
        scratch_shapes=scratch,
        name=name,
        **params(microseconds, vmem),
    )(*operands)


def chip_kernel(ids, mine, theirs, out):
    rows = out.shape[1]
    for block in range(CHIPS):
        at = slice(block * rows, (block + 1) * rows)
        out[block] = (mine[at].astype(F32) + theirs[at].astype(F32)).astype(BF16)


def total(blocks, low, rows):
    value = blocks[0, low : low + rows, :].astype(F32)
    for block in range(1, CHIPS):
        value = value + blocks[block, low : low + rows, :].astype(F32)
    return value.astype(BF16)


def chip_one_kernel(ids, mine, theirs, upper, out):
    for block in range(CHIPS):
        at = slice(block * LOWER_BLOCK, (block + 1) * LOWER_BLOCK)
        out[block, :UPPER_BLOCK, :] = upper[block]
        out[block, UPPER_BLOCK:, :] = (mine[at].astype(F32) + theirs[at].astype(F32)).astype(BF16)


def total_kernel(ids, blocks, out):
    value = total(blocks, 0, blocks.shape[1])
    for block in range(CHIPS):
        out[block] = value


def join_halves(ids, mine, theirs, packed, low):
    rows = packed.shape[1] // CHIPS
    for half, source in ((ids[2], mine), (1 - ids[2], theirs)):
        for block in range(CHIPS):
            packed[half, block * rows : (block + 1) * rows, :] = source[block, low : low + rows, :]


def last_kernel(
    factor, ids, mine, theirs, qkv, proj, up, down, merge, qkv_two, proj_two, up_two, down_two, lower, upper
):
    join_halves(ids, mine, theirs, upper, 0)
    for out, base in ((up_two, 0), (down_two, 4608), (proj_two, 9216), (merge, 13824)):
        out[...] = take(upper, base, out.shape[0], out.shape[1] // LANES) * factor
    for j in range(3):
        qkv_two[:, j * C2 : (j + 1) * C2] = take(upper, 10368 + j * 1152, C2, 3) * factor
    join_halves(ids, mine, theirs, lower, UPPER_BLOCK)
    joined = take(lower, 0, C1, 6) * factor
    qkv[...] = joined[:, : 3 * C1]
    proj[...] = joined[:, 3 * C1 :]
    up[...] = take(lower, 1152, C1, 6) * factor
    down[...] = take(lower, 2304, C1, 6) * factor


def assemble_kernel(ids, own, own_two, lon, lat, corner, place, place_two, tokens, two):
    arrived = jnp.concatenate([lon[...], lat[...], corner[...]], axis=0)
    cells = own[...] + nn(place[...], arrived)
    for row in range(12):
        tokens[row] = cells[row * 24 : (row + 1) * 24]
    cells = own_two[...] + nn(place_two[...], arrived)
    for level in range(2):
        two[:, 0, level * C2 : (level + 1) * C2] = cells[level * 72 : (level + 1) * 72]


def per_device(
    tokens, cotangent, bias_one, qkv_one, proj_one, up_one, down_one,
    merge_weight, bias_two, qkv_two, proj_two, up_two, down_two,
):
    lon = ("chip", "core")
    both = ("lat", "chip", "core")
    lats, lons = lax.axis_size("lat"), lax.axis_size(lon)
    ids = jnp.stack([lax.axis_index(name) for name in both]).astype(jnp.int32)
    factor = (WINDOW * lats * lons) ** -0.5
    from_right = [((i + 1) % lons, i) for i in range(lons)]
    to_right = [(i, (i + 1) % lons) for i in range(lons)]
    from_up = [(i, (i + 1) % lats) for i in range(lats)]
    to_up = [((i + 1) % lats, i) for i in range(lats)]
    down_one = down_one.T
    corner_in = [
        (i * lons + (j + 1) % lons, (i + 1) % lats * lons + j) for i in range(lats) for j in range(lons)
    ]
    corner_out = [
        ((i + 1) % lats * lons + j, i * lons + (j + 1) % lons) for i in range(lats) for j in range(lons)
    ]
    for_left, for_down = pack(tokens[0], cotangent[0])
    right = lax.ppermute(for_left, lon, from_right)
    up = lax.ppermute(for_down, "lat", from_up)
    diag = lax.ppermute(for_down, both, corner_in)

    bias_a, bias_b, bias_c = expand_bias(ids, bias_one, bias_two, bias_constants())
    select, gather, cot_select, strips, back_own, back_strips = constants()
    mask, mask_t, fold = blocks_of_heads()
    out_two, xw, grad_own, lon_strip, lat_strip, corner, mine_two, theirs_two = upper(
        ids, tokens[0], cotangent[0], right, up, diag, bias_a, bias_b, bias_c,
        qkv_one, proj_one, up_one, down_one, merge_weight, qkv_two, proj_two, up_two, down_two,
        select, gather, cot_select, strips, mask, mask_t, fold,
    )
    lon_strip = lax.ppermute(lon_strip, lon, to_right)
    lat_strip = lax.ppermute(lat_strip, "lat", to_up)
    corner = lax.ppermute(corner, both, corner_out)
    other_core = [(i, 1 - i) for i in range(2)]
    theirs_two = lax.ppermute(theirs_two, "core", other_core)
    result = lambda *dims: jax.ShapeDtypeStruct(dims, F32)
    blocks = lambda rows: jax.ShapeDtypeStruct((CHIPS, rows, LANES), BF16)
    chips = ("lat", "chip")
    packed_two = call(chip_kernel, "chip_two", 3, 16, blocks(UPPER_BLOCK), (ids, mine_two, theirs_two))
    to_tokens, to_two, place, place_two = output_constants()
    kept = lower_forward(xw, bias_a, bias_b, qkv_one, proj_one, up_one, mask, mask_t, fold)
    own_cells, own_two, lon_strip, lat_strip, corner, mine_one, theirs_one = lower(
        ids, out_two, grad_own, lon_strip, lat_strip, corner, *kept,
        qkv_one, proj_one, up_one, down_one,
        back_own, back_strips, to_tokens, to_two, mask, mask_t, fold,
    )
    theirs_one = lax.ppermute(theirs_one, "core", other_core)
    packed = call(
        chip_one_kernel, "chip_one", 1, 16, blocks(UPPER_BLOCK + LOWER_BLOCK),
        (ids, mine_one, theirs_one, packed_two),
    )
    packed = lax.all_to_all(packed, chips, 0, 0, tiled=True)
    lon_strip = lax.ppermute(lon_strip, lon, to_right)
    lat_strip = lax.ppermute(lat_strip, "lat", to_up)
    corner = lax.ppermute(corner, both, corner_out)
    summed = call(total_kernel, "total", 2, 16, blocks(UPPER_BLOCK + LOWER_BLOCK), (ids, packed))
    gathered = lax.all_to_all(summed, chips, 0, 0, tiled=True)
    weights = (qkv_one, proj_one, up_one, down_one, merge_weight, qkv_two, proj_two, up_two, down_two)
    sums = call(
        functools.partial(last_kernel, factor), "last", 6, 40, tuple(result(*w.shape) for w in weights),
        (ids, gathered, lax.ppermute(gathered, "core", other_core)),
        [
            pltpu.VMEM((2, CHIPS * LOWER_BLOCK, LANES), BF16),
            pltpu.VMEM((2, CHIPS * UPPER_BLOCK, LANES), BF16),
        ],
    )
    own_cells, *sums = lax.optimization_barrier((own_cells, *sums))
    grad_tokens, out_two = call(
        assemble_kernel, "assemble", 3, 8, (result(12, 24, 2 * C1), result(72, 1, 2 * C2)),
        (ids, own_cells, own_two, lon_strip, lat_strip, corner, place, place_two),
    )
    return (out_two.reshape(1, 6, 12, 2 * C2), grad_tokens[None], *sums[:3], sums[3].T, *sums[4:])


def solution(mesh):
    lats, lons = mesh.devices.shape
    mesh = Mesh(mesh.devices.reshape(lats, lons // 2, 2), ("lat", "chip", "core"))
    sharded, copied = P(None, "lat", ("chip", "core"), None), P()
    return jax.shard_map(
        per_device,
        mesh=mesh,
        in_specs=(sharded, sharded) + (copied,) * 11,
        out_specs=(sharded, sharded) + (copied,) * 9,
        check_vma=False,
    )
```

```python
import functools

import jax
import jax.numpy as jnp
import numpy as np
from jax import lax
from jax.experimental import pallas as pl
from jax.experimental.pallas import tpu as pltpu
from jax.sharding import Mesh, PartitionSpec as P

C1 = 192
C2 = 384
HEAD = 32
LEVELS = 2
WLAT = 6
WLON = 12
WINDOW = 144
REL = 2 * WLON - 1
COLUMN = LEVELS * WLAT
FACTOR = HEAD**-0.5
EPSILON = 1e-05
MASKED = -1e30
GROUPS_ONE = ((0, 4), (4, 2))
GROUPS_TWO = ((0, 4), (4, 4), (8, 4))
STRIPS = (112, 112, 48)
MIB = 1024 * 1024
SHIFT = (96, 96, 64)
SHIFT_TOKENS = (56, 56, 24)
LANES = 128
CHIPS = 64
UPPER_BLOCK = 128
LOWER_BLOCK = 32
F32 = jnp.float32
BF16 = jnp.bfloat16


def constants():
    select = np.zeros((2, 432, 288), np.float32)
    for col in range(36):
        half, source = (0, 6 + col) if col < 18 else (1, col - 18)
        for level in range(2):
            for a in range(6):
                select[level, col * 12 + level * 6 + a, half * 144 + a * 24 + source] = 1
    own = {}
    gather = np.zeros((3, 576, 432), np.float32)
    for pr in range(2):
        for pc in range(2):
            for out_col in range(12):
                for level in range(2):
                    for out_row in range(6):
                        row, col = 3 + 2 * out_row + pr, 6 + 2 * out_col + pc
                        place = (pr * 2 + pc) * 144 + out_col * 12 + level * 6 + out_row
                        gather[row // 6, place, col * 12 + level * 6 + row % 6] = 1
                        own[row, col, level] = place
    cot_select = np.zeros((144, 288), np.float32)
    for out_col in range(12):
        for out_row in range(6):
            for level in range(2):
                up, right = out_row < 3, out_col >= 6
                block = (2 if up else 0) + (1 if right else 0)
                col = out_col - 6 if right else 6 + out_col
                place = out_col * 12 + level * 6 + out_row
                cot_select[place, block * 72 + out_row % 3 * 24 + level * 12 + col] = 1
    strips = np.zeros((sum(STRIPS), 576), np.float32)
    back_own = np.zeros((576, 576), np.float32)
    back_strips = np.zeros((576, sum(STRIPS)), np.float32)
    for row in range(6, 18):
        for col in range(24):
            for level in range(2):
                target = (row - 6) // 6 * 288 + col * 12 + level * 6 + row % 6
                if row <= 14 and col >= 6:
                    back_own[target, own[row, col, level]] = 1
                    continue
                if row <= 14:
                    place = (row - 6) * 12 + col * 2 + level
                    sent = (row, 24 + col, level)
                elif col >= 6:
                    place = STRIPS[0] + (row - 15) * 36 + (col - 6) * 2 + level
                    sent = (row - 12, col, level)
                else:
                    place = STRIPS[0] + STRIPS[1] + (row - 15) * 12 + col * 2 + level
                    sent = (row - 12, 24 + col, level)
                back_strips[target, place] = 1
                strips[place, own[sent]] = 1
    return tuple(jnp.asarray(v, BF16) for v in (select, gather, cot_select, strips, back_own, back_strips))


def output_constants():
    starts = (0, SHIFT[0], SHIFT[0] + SHIFT[1])
    tokens = np.zeros((2, 288 + sum(SHIFT_TOKENS), 576), np.float32)
    place = np.zeros((288, sum(SHIFT)), np.float32)
    two = np.zeros((144 + sum(SHIFT) - sum(SHIFT_TOKENS), WINDOW), np.float32)
    place_two = np.zeros((144, sum(SHIFT)), np.float32)

    def strip(row, col, rows, cols):
        if row < rows:
            return (None, row, col - cols) if col >= cols else (0, row, col)
        return (1, row - rows, col - cols) if col >= cols else (2, row - rows, col)

    for row in range(12):
        for col in range(24):
            kind, sub_row, sub_col = strip(row, col, 9, 6)
            source_row = row + 3 if row < 9 else row - 9
            source_col = col - 6 if col >= 6 else col + 18
            if kind is None:
                target = row * 24 + col
            else:
                at = sub_row * (18 if kind == 1 else 6) + sub_col
                target = 288 + sum(SHIFT_TOKENS[:kind]) + at
                place[row * 24 + col, starts[kind] + at] = 1
            for level in range(2):
                source = source_row // 6 * 288 + source_col * 12 + level * 6 + source_row % 6
                tokens[level, target, source] = 1
    for row in range(6):
        for col in range(12):
            kind, sub_row, sub_col = strip(row, col, 3, 6)
            source_row = row + 3 if row < 3 else row - 3
            source_col = col - 6 if col >= 6 else col + 6
            for level in range(2):
                if kind is None:
                    target = level * 72 + row * 12 + col
                else:
                    at = level * 18 + sub_row * 6 + sub_col
                    target = 144 + kind * 40 + at
                    place_two[level * 72 + row * 12 + col, starts[kind] + SHIFT_TOKENS[kind] + at] = 1
                two[target, source_col * 12 + level * 6 + source_row] = 1
    return tuple(jnp.asarray(v, BF16) for v in (tokens, two, place, place_two))


def bias_constants():
    z1, z2, a1, a2, r = (v.reshape(-1) for v in np.indices((LEVELS, LEVELS, WLAT, WLAT, REL)))
    half = WLAT // 2
    kind = np.where((a1 < half) & (a2 < half), 0, np.where((a1 >= half) & (a2 >= half), 1, 2))
    codes = np.stack([kind, z2, a2 + 2 * (1 - z2), r * COLUMN + z1 * WLAT + a1])
    return jnp.asarray(codes, F32)


def blocks_of_heads():
    mask = (np.arange(576)[:, None] // WINDOW == np.arange(128)[None] // HEAD).astype(np.float32)
    fold = (np.arange(WINDOW)[:, None] == np.arange(576)[None] % WINDOW).astype(np.float32)
    return tuple(jnp.asarray(v, BF16) for v in (mask, mask.T, fold))


def blocks_of_pairs():
    masks = []
    for heads in (4, 2):
        row, lane = np.arange(heads * WINDOW)[:, None], np.arange(2 * heads * HEAD)[None]
        same = row // WINDOW == lane % (heads * HEAD) // HEAD
        part = (row % WINDOW >= WINDOW // 2) == (lane >= heads * HEAD)
        masks += [(same & part).astype(np.float32), (same & part).astype(np.float32).T]
    return tuple(jnp.asarray(v, BF16) for v in masks)


def params(microseconds, vmem):
    return {
        "compiler_params": pltpu.CompilerParams(vmem_limit_bytes=vmem * MIB),
        "cost_estimate": pl.CostEstimate(
            flops=int(microseconds * 1e9), bytes_accessed=int(microseconds * 3e6), transcendentals=0
        ),
    }


def nn(left, right):
    return jnp.dot(left, right, preferred_element_type=F32)


def nt(left, right):
    return lax.dot_general(left, right, (((1,), (1,)), ((), ())), preferred_element_type=F32)


def tn(left, right):
    return lax.dot_general(left, right, (((0,), (0,)), ((), ())), preferred_element_type=F32)


def layer_norm(values):
    average = jnp.mean(values, axis=-1, keepdims=True)
    centred = values - average
    scale = lax.rsqrt(jnp.mean(centred * centred, axis=-1, keepdims=True) + EPSILON)
    return centred * scale, scale


def layer_norm_back(grad, normed, scale):
    first = jnp.mean(grad, axis=-1, keepdims=True)
    second = jnp.mean(grad * normed, axis=-1, keepdims=True)
    return scale * (grad - first - normed * second)


GELU_A = (2.0 / np.pi) ** 0.5
GELU_B = 0.044715


def gelu(values):
    tanh = jnp.tanh(GELU_A * (values + GELU_B * (values * values * values)))
    return 0.5 * values * (1.0 + tanh)


def gelu_both(values):
    square = values * values
    tanh = jnp.tanh(GELU_A * values * (1.0 + GELU_B * square))
    half = 0.5 * (1.0 + tanh)
    slope = half + 0.5 * values * (1.0 - tanh * tanh) * (GELU_A * (1.0 + 3.0 * GELU_B * square))
    return values * half, slope


def spread(values, mask, heads):
    return jnp.concatenate([values] * heads, axis=0) * mask[: heads * WINDOW, : heads * HEAD]


def pull(left, right, mask_t, fold, heads):
    both = tn(left, right).astype(BF16) * mask_t[: heads * HEAD, : heads * WINDOW]
    return nt(fold[:, : heads * WINDOW], both)


def attend(parts, mask, mask_t, fold):
    masks = [
        part[5] if len(part) > 5 else (mask[: part[4] * WINDOW, : part[4] * HEAD], mask_t[: part[4] * HEAD, : part[4] * WINDOW])
        for part in parts
    ]
    scores = [
        nt(part[1], jnp.concatenate([part[0]] * part[4], axis=0) * own[0]) * FACTOR + part[3]
        for part, own in zip(parts, masks)
    ]
    powers = [jnp.exp(score - jnp.max(score, axis=0, keepdims=True)) for score in scores]
    chances = [power * (1.0 / jnp.sum(power, axis=0, keepdims=True)) for power in powers]
    taken = [
        nt(fold[:, : part[4] * WINDOW], tn(part[2], chance.astype(BF16)).astype(BF16) * own[1])
        for part, own, chance in zip(parts, masks, chances)
    ]
    return taken, chances


def attend_back(parts, mask, mask_t, fold):
    grads = [spread(part[4], mask, part[5]) for part in parts]
    grad_chances = [nt(part[2], grad) for part, grad in zip(parts, grads)]
    grad_values = [nn(part[3].astype(BF16), grad) for part, grad in zip(parts, grads)]
    products = [grad * part[3] for part, grad in zip(parts, grad_chances)]
    grad_scores = [
        ((product - part[3] * jnp.sum(product, axis=0, keepdims=True)) * FACTOR).astype(BF16)
        for part, product in zip(parts, products)
    ]
    grad_keys = [nn(grad, spread(part[0], mask, part[5])) for part, grad in zip(parts, grad_scores)]
    grad_queries = [
        pull(part[1], grad, mask_t, fold, part[5]) for part, grad in zip(parts, grad_scores)
    ]
    return grad_queries, grad_keys, grad_values


SPANS = (((0, 896), (1536, 2560)), ((768, 1664), (2432, 3312)))


def bias_kernel(ids, one, two, codes, first_ref, second_ref, two_out_ref, pieces, table):
    band = ids[0]
    kind, level_of, row_of, place_of = (codes[i : i + 1, :] for i in range(4))
    places = lax.broadcasted_iota(jnp.int32, (REL * COLUMN, codes.shape[1]), 0).astype(F32)
    lanes = jnp.where(places == place_of, 1.0, 0.0).astype(BF16)
    row = lax.broadcasted_iota(jnp.int32, (8, codes.shape[1]), 0).astype(F32)

    def window(source, index):
        count = source.shape[0] - 1
        index = lax.rem(index + count, count)
        mixed = jnp.where(
            kind == 0.0, source[count], jnp.where(kind == 1.0, source[0], MASKED)
        )
        return jnp.where(index == 0, mixed, source[index])

    values = [
        window(one, 2 * band - 1), window(one, 2 * band), window(one, 2 * band + 1), window(two, band)
    ]
    heads = sum(value.shape[0] for value in values)
    for level in range(2):
        slot = 0
        rows = (row == row_of) & (level_of == float(level))
        for value in values:
            high = value.astype(BF16).astype(F32)
            low = value - high
            for h in range(0, value.shape[0], 2):
                for piece, taken in enumerate((high, low)):
                    at = 0
                    for start, stop in SPANS[level]:
                        chosen = rows[:, start:stop]
                        pair = [
                            jnp.where(chosen, taken[h + i : h + i + 1, start:stop], 0.0) for i in range(2)
                        ]
                        pieces[piece, (slot + h) * 8 : (slot + h) * 8 + 16, at : at + stop - start] = (
                            jnp.concatenate(pair, axis=0).astype(BF16)
                        )
                        at += stop - start
            slot += value.shape[0]
        total = None
        for piece in range(2):
            at = 0
            for start, stop in SPANS[level]:
                term = nt(pieces[piece, :, at : at + stop - start], lanes[:, start:stop])
                total = term if total is None else total + term
                at += stop - start
        for h in range(heads):
            table[h, level * 8 : level * 8 + 8, :] = total[h * 8 : h * 8 + 8]

    for base, count, groups, targets in (
        (0, 3, GROUPS_ONE, (first_ref, second_ref)),
        (18, 1, GROUPS_TWO, (two_out_ref, two_out_ref, two_out_ref)),
    ):
        for row in range(count):
            for index, (start, heads) in enumerate(groups):
                target = targets[index]
                place = row if count == 3 else index
                which = [base + row * 6 + start + h for h in range(heads)]
                for o2 in range(WLON):
                    left = (WLON - 1 - o2) * COLUMN
                    piece = [table[h, 2 : 2 + COLUMN, left : left + WINDOW] for h in which]
                    target[place, o2 * COLUMN : (o2 + 1) * COLUMN, :] = jnp.concatenate(piece, axis=1)


def expand_bias(*operands):
    return pl.pallas_call(
        bias_kernel,
        in_specs=specs(len(operands)),
        out_shape=(
            jax.ShapeDtypeStruct((3, WINDOW, 576), F32),
            jax.ShapeDtypeStruct((3, WINDOW, 288), F32),
            jax.ShapeDtypeStruct((3, WINDOW, 576), F32),
        ),
        scratch_shapes=[
            pltpu.VMEM((2, 240, 1920), BF16),
            pltpu.VMEM((30, 16, REL * COLUMN), F32),
        ],
        **params(7, 24),
        name="bias_expand",
    )(*operands)


def pack_kernel(tokens, cot, right_ref, up_ref):
    for out, row, cot_row in ((right_ref, 0, 0), (up_ref, 3, 3)):
        out[:9] = tokens[row : row + 9]
        for r in range(3):
            value = cot[cot_row + r].astype(F32)
            out[9 + r] = jnp.concatenate([value[:, :C2], value[:, C2:]], axis=0).astype(BF16)


def pack(tokens, cot):
    shape = jax.ShapeDtypeStruct((12, 24, 2 * C1), BF16)
    return pl.pallas_call(
        pack_kernel, out_shape=(shape, shape), name="pack", **params(2, 8)
    )(tokens, cot)


def put(packed, base, value):
    half, count = packed.shape[1], value.shape[0]
    for j in range(value.shape[1] // LANES):
        start, stop = base + j * count, base + (j + 1) * count
        lanes = value[:, j * LANES : (j + 1) * LANES]
        for part in range(2):
            low, high = max(start, part * half), min(stop, (part + 1) * half)
            if low < high:
                packed[part, low - part * half : high - part * half, :] = lanes[low - start : high - start]
    return base + value.shape[0] * value.shape[1] // LANES


def take(packed, base, count, columns):
    half, lanes = packed.shape[1], []
    for j in range(columns):
        start, stop, rows = base + j * count, base + (j + 1) * count, []
        for part in range(2):
            low, high = max(start, part * half), min(stop, (part + 1) * half)
            if low < high:
                rows.append(packed[part, low - part * half : high - part * half, :])
        lanes.append(rows[0] if len(rows) == 1 else jnp.concatenate(rows, axis=0))
    return jnp.concatenate(lanes, axis=1).astype(F32)


def send_half(ids, packed, half, mine_ref, theirs_ref, sems, start):
    for target, own in ((mine_ref, half), (theirs_ref, 1 - half)):

        @pl.when(ids[2] == own)
        def _():
            copy = pltpu.make_async_copy(packed.at[half], target, sems.at[half])
            if start:
                copy.start()
            else:
                copy.wait()


def upper_kernel(
    ids, own, cot_own, right, up, diag,
    bias_a, bias_b, bias_two,
    qkv_one, proj_one, up_one, down_one, merge, qkv_two, proj_two, up_two, down_two,
    select, gather, cot_select, strips, mask_ref, mask_t_ref, fold_ref,
    pair_four, pair_four_t, pair_two, pair_two_t,
    out_ref, xw_ref, grad_ref, lon_ref, lat_ref, corner_ref, mine_ref, theirs_ref,
    q_ref, k_ref, v_ref, att_ref, xm_ref, am_ref, one_ref, p_ref, packed, sems,
):
    mask, mask_t, fold = mask_ref[...], mask_t_ref[...], fold_ref[...]

    def rows_of(block, start, count):
        return [block[start + r].astype(F32) for r in range(count)]

    for wr in range(3):
        if wr == 0:
            left, other = rows_of(up, 0, 6), rows_of(diag, 0, 6)
        elif wr == 1:
            left = rows_of(up, 6, 3) + rows_of(own, 0, 3)
            other = rows_of(diag, 6, 3) + rows_of(right, 0, 3)
        else:
            left, other = rows_of(own, 3, 6), rows_of(right, 3, 6)
        source = jnp.concatenate(left + other, axis=0).astype(BF16)
        cells = nn(select[0], source[:, :C1]) + nn(select[1], source[:, C1:])
        xw_ref[wr] = cells.astype(BF16)
        normed = layer_norm(cells)[0].astype(BF16)
        projected = nn(normed, qkv_one[...]).astype(BF16)
        q_ref[wr] = projected[:, :C1]
        k_ref[wr] = projected[:, C1 : 2 * C1]
        v_ref[wr] = projected[:, 2 * C1 :]

    @pl.loop(0, 3)
    def _(wr):
        first, second, third = (slice(wc * WINDOW, (wc + 1) * WINDOW) for wc in range(3))
        parts = []
        for start, heads in GROUPS_ONE:
            lanes = slice(start * HEAD, (start + heads) * HEAD)
            bias = bias_a[wr] if heads == 4 else bias_b[wr]
            refs = (q_ref, k_ref, v_ref)
            pair = (pair_four[...], pair_four_t[...]) if heads == 4 else (pair_two[...], pair_two_t[...])
            joined = [
                jnp.concatenate([ref[wr, third, lanes], ref[wr, first, lanes]], axis=1) for ref in refs
            ]
            parts.append((*(ref[wr, second, lanes] for ref in refs), bias, heads))
            parts.append((*joined, bias, heads, pair))
        taken, _ = attend(parts, mask, mask_t, fold)
        for index, (start, heads) in enumerate(GROUPS_ONE):
            lanes, width = slice(start * HEAD, (start + heads) * HEAD), heads * HEAD
            att_ref[wr, second, lanes] = taken[2 * index].astype(BF16)
            att_ref[wr, third, lanes] = taken[2 * index + 1][:, :width].astype(BF16)
            att_ref[wr, first, lanes] = taken[2 * index + 1][:, width:].astype(BF16)

    xm_ref[...] = nn(gather[0], xw_ref[0]) + nn(gather[1], xw_ref[1]) + nn(gather[2], xw_ref[2])
    am_ref[...] = (
        nn(gather[0], att_ref[0]) + nn(gather[1], att_ref[1]) + nn(gather[2], att_ref[2])
    ).astype(BF16)

    for half in range(2):
        rows = slice(half * 288, (half + 1) * 288)
        middle = xm_ref[rows, :] + nn(am_ref[rows, :], proj_one[...])
        normed = layer_norm(middle)[0].astype(BF16)
        active = gelu(nn(normed, up_one[...])).astype(BF16)
        one_ref[rows, :] = middle + nt(active, down_one[...])

    parts = [one_ref[g * WINDOW : (g + 1) * WINDOW, :] for g in range(4)]
    average = sum(jnp.sum(part, axis=-1, keepdims=True) for part in parts) / (4 * C1)
    spread_of = sum(
        jnp.sum((part - average) * (part - average), axis=-1, keepdims=True) for part in parts
    ) / (4 * C1)
    merge_scale = lax.rsqrt(spread_of + EPSILON)
    merged = [((part - average) * merge_scale) for part in parts]
    merged_low = [part.astype(BF16) for part in merged]
    grid = sum(nn(merged_low[g], merge[g * C1 : (g + 1) * C1, :]) for g in range(4))

    normed_full, scale = layer_norm(grid)
    normed = normed_full.astype(BF16)
    q, k, v = (nn(normed, qkv_two[:, j * C2 : (j + 1) * C2]).astype(BF16) for j in range(3))
    lanes_of = [slice(start * HEAD, (start + heads) * HEAD) for start, heads in GROUPS_TWO]
    taken, chances = attend(
        [(q[:, at], k[:, at], v[:, at], bias_two[index], 4) for index, at in enumerate(lanes_of)],
        mask, mask_t, fold,
    )
    for index in range(3):
        p_ref[index] = chances[index]
    attended = jnp.concatenate([value.astype(BF16) for value in taken], axis=1)
    middle = grid + nn(attended, proj_two[...])
    normed_two_full, scale_two = layer_norm(middle)
    normed_two = normed_two_full.astype(BF16)
    active, slope = gelu_both(nn(normed_two, up_two[...]))
    active = active.astype(BF16)
    out_ref[...] = middle + nn(active, down_two[...])

    cot = []
    for r in range(3):
        value = cot_own[r].astype(F32)
        cot += [value[:, :C2], value[:, C2:]]
    for block in (right, up, diag):
        cot += rows_of(block, 9, 3)
    grad = nn(cot_select[...], jnp.concatenate(cot, axis=0).astype(BF16))
    grad_low = grad.astype(BF16)
    put(packed, 4608, tn(active, grad_low).astype(BF16))
    grad_raised = (nt(grad_low, down_two[...]) * slope).astype(BF16)
    put(packed, 0, tn(normed_two, grad_raised).astype(BF16))
    send_half(ids, packed, 0, mine_ref, theirs_ref, sems, True)
    grad_middle = grad + layer_norm_back(nt(grad_raised, up_two[...]), normed_two_full, scale_two)
    grad_middle_low = grad_middle.astype(BF16)
    put(packed, 9216, tn(attended, grad_middle_low).astype(BF16))
    grad_attended = nt(grad_middle_low, proj_two[...]).astype(BF16)
    pieces = attend_back(
        [
            (q[:, at], k[:, at], v[:, at], p_ref[index], grad_attended[:, at], 4)
            for index, at in enumerate(lanes_of)
        ],
        mask, mask_t, fold,
    )
    grad_normed = None
    for j in range(3):
        part = jnp.concatenate([value.astype(BF16) for value in pieces[j]], axis=1)
        put(packed, 10368 + j * 1152, tn(normed, part).astype(BF16))
        term = nt(part, qkv_two[:, j * C2 : (j + 1) * C2])
        grad_normed = term if grad_normed is None else grad_normed + term
    grad_grid = (grad_middle + layer_norm_back(grad_normed, normed_full, scale)).astype(BF16)

    grad_parts = []
    grad_merge = [tn(merged_low[g], grad_grid).astype(BF16) for g in range(4)]
    put(packed, 13824, jnp.concatenate(grad_merge, axis=0))
    packed[1, 16128 - packed.shape[1] :, :] = jnp.zeros((256, LANES), BF16)
    send_half(ids, packed, 1, mine_ref, theirs_ref, sems, True)
    for g in range(4):
        grad_parts.append(nt(grad_grid, merge[g * C1 : (g + 1) * C1, :]))
    first = sum(jnp.sum(part, axis=-1, keepdims=True) for part in grad_parts) / (4 * C1)
    second = sum(
        jnp.sum(part * kept, axis=-1, keepdims=True) for part, kept in zip(grad_parts, merged)
    ) / (4 * C1)
    for g in range(4):
        grad_ref[g * WINDOW : (g + 1) * WINDOW, :] = (
            merge_scale * (grad_parts[g] - first - merged[g] * second)
        ).astype(BF16)
    sent = nn(strips[...], grad_ref[...]).astype(BF16)
    lon_ref[...] = sent[: STRIPS[0]]
    lat_ref[...] = sent[STRIPS[0] : STRIPS[0] + STRIPS[1]]
    corner_ref[...] = sent[STRIPS[0] + STRIPS[1] :]
    for half in range(2):
        send_half(ids, packed, half, mine_ref, theirs_ref, sems, False)


def packed_shape(block):
    return jax.ShapeDtypeStruct((CHIPS * block, LANES), BF16)


def specs(count):
    vmem = pl.BlockSpec(memory_space=pltpu.VMEM)
    return [pl.BlockSpec(memory_space=pltpu.SMEM)] + [vmem] * (count - 1)


def out_specs(count, last_any):
    vmem, left = pl.BlockSpec(memory_space=pltpu.VMEM), pl.BlockSpec(memory_space=pl.ANY)
    return tuple([vmem] * (count - last_any) + [left] * last_any)


def upper(*operands):
    shape = jax.ShapeDtypeStruct
    return pl.pallas_call(
        upper_kernel,
        in_specs=specs(len(operands)),
        out_specs=out_specs(8, 2),
        out_shape=(
            shape((WINDOW, C2), F32),
            shape((3, 432, C1), BF16),
            shape((576, C1), BF16),
            shape((STRIPS[0], C1), BF16),
            shape((STRIPS[1], C1), BF16),
            shape((STRIPS[2], C1), BF16),
            packed_shape(UPPER_BLOCK),
            packed_shape(UPPER_BLOCK),
        ),
        scratch_shapes=[
            pltpu.VMEM((3, 432, C1), BF16),
            pltpu.VMEM((3, 432, C1), BF16),
            pltpu.VMEM((3, 432, C1), BF16),
            pltpu.VMEM((3, 432, C1), BF16),
            pltpu.VMEM((576, C1), F32),
            pltpu.VMEM((576, C1), BF16),
            pltpu.VMEM((576, C1), F32),
            pltpu.VMEM((3, WINDOW, 576), F32),
            pltpu.VMEM((2, CHIPS * UPPER_BLOCK, LANES), BF16),
            pltpu.SemaphoreType.DMA((2,)),
        ],
        **params(25, 40),
        name="upper",
    )(*operands)


def window_places(row, pa_ref, pb_ref):
    return [
        (
            pl.ds(pl.multiple_of(row * 288 + wc * WINDOW, WINDOW), WINDOW),
            slice(start * HEAD, (start + heads) * HEAD),
            heads,
            (pa_ref if heads == 4 else pb_ref, row * 2 + wc),
        )
        for wc in range(2)
        for start, heads in GROUPS_ONE
    ]


def halves(value):
    high = value.astype(BF16)
    return high, (value - high.astype(F32)).astype(BF16)


def lower_forward_kernel(
    xw, bias_a, bias_b, qkv_one, proj_one, up_one, mask_ref, mask_t_ref, fold_ref,
    normed_ref, full_ref, scale_ref, q_ref, k_ref, v_ref, pa_ref, pb_ref, att_ref,
    normed_two_ref, full_two_ref, scale_two_ref, act_ref, slope_ref,
):
    mask, mask_t, fold = mask_ref[...], mask_t_ref[...], fold_ref[...]
    row_slices = [slice(row * 288, (row + 1) * 288) for row in range(2)]
    for row, rows in enumerate(row_slices):
        full, scale = layer_norm(xw[1 + row, :288, :].astype(F32))
        full_ref[rows, :] = full
        scale_ref[rows, :] = scale
        normed = full.astype(BF16)
        normed_ref[rows, :] = normed
        projected = nn(normed, qkv_one[...]).astype(BF16)
        q_ref[rows, :] = projected[:, :C1]
        k_ref[rows, :] = projected[:, C1 : 2 * C1]
        v_ref[rows, :] = projected[:, 2 * C1 :]

    @pl.loop(0, 2)
    def _(row):
        places = window_places(row, pa_ref, pb_ref)
        parts = [
            (
                q_ref[rows, at], k_ref[rows, at], v_ref[rows, at],
                bias_a[1 + row] if heads == 4 else bias_b[1 + row], heads,
            )
            for rows, at, heads, _ in places
        ]
        taken, chances = attend(parts, mask, mask_t, fold)
        for (rows, at, _, (kept, window)), value, chance in zip(places, taken, chances):
            att_ref[rows, at] = value.astype(BF16)
            kept[window] = chance

    for row, rows in enumerate(row_slices):
        middle = xw[1 + row, :288, :].astype(F32) + nn(att_ref[rows, :], proj_one[...])
        full, scale = layer_norm(middle)
        full_two_ref[rows, :] = full
        scale_two_ref[rows, :] = scale
        normed_two = full.astype(BF16)
        normed_two_ref[rows, :] = normed_two
        active, slope = gelu_both(nn(normed_two, up_one[...]))
        act_ref[rows, :] = active.astype(BF16)
        slope_ref[rows, :] = slope


def lower_forward(*operands):
    shape = jax.ShapeDtypeStruct
    wide, full, scale = shape((576, C1), BF16), shape((576, C1), F32), shape((576, 1), F32)
    return pl.pallas_call(
        lower_forward_kernel,
        out_shape=(
            wide, full, scale, wide, wide, wide,
            shape((4, WINDOW, 576), F32), shape((4, WINDOW, 288), F32), wide,
            wide, full, scale, shape((576, 768), BF16), shape((576, 768), F32),
        ),
        name="lower_forward",
        **params(5, 32),
    )(*operands)


def lower_kernel(
    ids, own, lon, lat, corner,
    normed_ref, q_ref, k_ref, v_ref, pa_ref, pb_ref, att_ref,
    normed_two_ref, full_two_ref, scale_two_ref, act_ref, slope_ref,
    proj_one, up_one, down_one, back_own, back_strips, mask_ref, mask_t_ref, fold_ref,
    gm_ref, gq_ref, gk_ref, gv_ref, mine_ref, theirs_ref,
    gs_ref, raised_ref, gml_ref, ga_ref, packed, sems,
):
    mask, mask_t, fold = mask_ref[...], mask_t_ref[...], fold_ref[...]
    arrived = jnp.concatenate([lon[...], lat[...], corner[...]], axis=0)
    gs_ref[...] = nn(back_own[...], own[...]) + nn(back_strips[...], arrived)
    row_slices = [slice(row * 288, (row + 1) * 288) for row in range(2)]

    for rows in row_slices:
        grad = gs_ref[rows, :]
        grad_raised = (nn(grad.astype(BF16), down_one[...]) * slope_ref[rows, :]).astype(BF16)
        raised_ref[rows, :] = grad_raised
        grad_middle = grad + layer_norm_back(
            nt(grad_raised, up_one[...]), full_two_ref[rows, :], scale_two_ref[rows, :]
        )
        gm_ref[rows, :] = grad_middle
        low = grad_middle.astype(BF16)
        gml_ref[rows, :] = low
        ga_ref[rows, :] = nt(low, proj_one[...]).astype(BF16)

    @pl.loop(0, 2)
    def _(row):
        places = window_places(row, pa_ref, pb_ref)
        parts = [
            (q_ref[rows, at], k_ref[rows, at], v_ref[rows, at], kept[window], ga_ref[rows, at], heads)
            for rows, at, heads, (kept, window) in places
        ]
        grads = attend_back(parts, mask, mask_t, fold)
        for target, values in zip((gq_ref, gk_ref, gv_ref), grads):
            for (rows, at, _, _), value in zip(places, values):
                target[rows, at] = value.astype(BF16)

    normed = normed_ref[...]
    grads = [tn(normed, ref[...]) for ref in (gq_ref, gk_ref, gv_ref)]
    grads = jnp.concatenate(grads + [tn(att_ref[...], gml_ref[...])], axis=1)
    put(packed, 0, grads.astype(BF16))
    put(packed, 1152, tn(normed_two_ref[...], raised_ref[...]).astype(BF16))
    put(packed, 2304, tn(gs_ref[...].astype(BF16), act_ref[...]).astype(BF16))
    packed[1, 3456 - packed.shape[1] :, :] = jnp.zeros((640, LANES), BF16)
    for half in range(2):
        send_half(ids, packed, half, mine_ref, theirs_ref, sems, True)
    for half in range(2):
        send_half(ids, packed, half, mine_ref, theirs_ref, sems, False)


def finish_kernel(
    ids, gm_ref, gq_ref, gk_ref, gv_ref, full_ref, scale_ref, out_two, qkv_one, to_tokens, to_two,
    out_ref, out_two_ref, lon_ref, lat_ref, corner_ref, gx_ref,
):
    for row in range(2):
        rows = slice(row * 288, (row + 1) * 288)
        grad_normed = (
            nt(gq_ref[rows, :], qkv_one[:, :C1])
            + nt(gk_ref[rows, :], qkv_one[:, C1 : 2 * C1])
            + nt(gv_ref[rows, :], qkv_one[:, 2 * C1 :])
        )
        gx_ref[rows, :] = gm_ref[rows, :] + layer_norm_back(
            grad_normed, full_ref[rows, :], scale_ref[rows, :]
        )
    high, low = halves(gx_ref[...])
    cells = jnp.concatenate(
        [nn(to_tokens[level], high) + nn(to_tokens[level], low) for level in range(2)], axis=1
    )
    high, low = halves(out_two[...])
    two = nn(to_two[...], high) + nn(to_two[...], low)
    out_ref[...] = cells[:288]
    out_two_ref[...] = two[:144]
    at = 288
    for kind, ref in enumerate((lon_ref, lat_ref, corner_ref)):
        count = SHIFT_TOKENS[kind]
        strip = [cells[at : at + count], two[144 + kind * 40 : 144 + (kind + 1) * 40]]
        ref[...] = jnp.concatenate(strip, axis=0).astype(BF16)
        at += count


def lower(*operands):
    shape = jax.ShapeDtypeStruct
    wide = shape((576, C1), BF16)
    return pl.pallas_call(
        lower_kernel,
        in_specs=specs(len(operands)),
        out_specs=out_specs(6, 2),
        out_shape=(
            shape((576, C1), F32), wide, wide, wide,
            packed_shape(LOWER_BLOCK), packed_shape(LOWER_BLOCK),
        ),
        scratch_shapes=[
            pltpu.VMEM((576, C1), F32),
            pltpu.VMEM((576, 768), BF16),
            pltpu.VMEM((576, C1), BF16),
            pltpu.VMEM((576, C1), BF16),
            pltpu.VMEM((2, CHIPS * LOWER_BLOCK, LANES), BF16),
            pltpu.SemaphoreType.DMA((2,)),
        ],
        name="lower",
        **params(10, 32),
    )(*operands)


def call(kernel, name, microseconds, vmem, out_shape, operands, scratch=()):
    return pl.pallas_call(
        kernel,
        in_specs=specs(len(operands)),
        out_shape=out_shape,
        scratch_shapes=scratch,
        name=name,
        **params(microseconds, vmem),
    )(*operands)


def chip_kernel(ids, mine_two, theirs_two, mine_one, theirs_one, out):
    for low, mine, theirs in ((0, mine_two, theirs_two), (UPPER_BLOCK, mine_one, theirs_one)):
        rows = mine.shape[0] // CHIPS
        for block in range(CHIPS):
            at = slice(block * rows, (block + 1) * rows)
            value = mine[at].astype(F32) + theirs[at].astype(F32)
            out[block, low : low + rows, :] = value.astype(BF16)


def total(blocks, low, rows):
    value = blocks[0, low : low + rows, :].astype(F32)
    for block in range(1, CHIPS):
        value = value + blocks[block, low : low + rows, :].astype(F32)
    return value.astype(BF16)


def total_kernel(ids, blocks, out):
    value = total(blocks, 0, blocks.shape[1])
    for block in range(CHIPS):
        out[block] = value


def join_halves(ids, mine, theirs, packed, low):
    rows = packed.shape[1] // CHIPS
    for half, source in ((ids[2], mine), (1 - ids[2], theirs)):
        for block in range(CHIPS):
            packed[half, block * rows : (block + 1) * rows, :] = source[block, low : low + rows, :]


def last_kernel(
    factor, ids, mine, theirs, qkv, proj, up, down, merge, qkv_two, proj_two, up_two, down_two, lower, upper
):
    join_halves(ids, mine, theirs, upper, 0)
    for out, base in ((up_two, 0), (down_two, 4608), (proj_two, 9216), (merge, 13824)):
        out[...] = take(upper, base, out.shape[0], out.shape[1] // LANES) * factor
    for j in range(3):
        qkv_two[:, j * C2 : (j + 1) * C2] = take(upper, 10368 + j * 1152, C2, 3) * factor
    join_halves(ids, mine, theirs, lower, UPPER_BLOCK)
    joined = take(lower, 0, C1, 6) * factor
    qkv[...] = joined[:, : 3 * C1]
    proj[...] = joined[:, 3 * C1 :]
    up[...] = take(lower, 1152, C1, 6) * factor
    down[...] = take(lower, 2304, C1, 6) * factor


def assemble_kernel(ids, own, own_two, lon, lat, corner, place, place_two, tokens, two):
    arrived = jnp.concatenate([lon[...], lat[...], corner[...]], axis=0)
    cells = own[...] + nn(place[...], arrived)
    for row in range(12):
        tokens[row] = cells[row * 24 : (row + 1) * 24]
    cells = own_two[...] + nn(place_two[...], arrived)
    for level in range(2):
        two[:, 0, level * C2 : (level + 1) * C2] = cells[level * 72 : (level + 1) * 72]


def per_device(
    tokens, cotangent, bias_one, qkv_one, proj_one, up_one, down_one,
    merge_weight, bias_two, qkv_two, proj_two, up_two, down_two,
):
    lon = ("chip", "core")
    both = ("lat", "chip", "core")
    lats, lons = lax.axis_size("lat"), lax.axis_size(lon)
    ids = jnp.stack([lax.axis_index(name) for name in both]).astype(jnp.int32)
    factor = (WINDOW * lats * lons) ** -0.5
    from_right = [((i + 1) % lons, i) for i in range(lons)]
    to_right = [(i, (i + 1) % lons) for i in range(lons)]
    from_up = [(i, (i + 1) % lats) for i in range(lats)]
    to_up = [((i + 1) % lats, i) for i in range(lats)]
    down_one = down_one.T
    corner_in = [
        (i * lons + (j + 1) % lons, (i + 1) % lats * lons + j) for i in range(lats) for j in range(lons)
    ]
    corner_out = [
        ((i + 1) % lats * lons + j, i * lons + (j + 1) % lons) for i in range(lats) for j in range(lons)
    ]
    for_left, for_down = pack(tokens[0], cotangent[0])
    right = lax.ppermute(for_left, lon, from_right)
    up = lax.ppermute(for_down, "lat", from_up)
    diag = lax.ppermute(for_down, both, corner_in)

    bias_a, bias_b, bias_c = expand_bias(ids, bias_one, bias_two, bias_constants())
    select, gather, cot_select, strips, back_own, back_strips = constants()
    mask, mask_t, fold = blocks_of_heads()
    out_two, xw, grad_own, lon_strip, lat_strip, corner, mine_two, theirs_two = upper(
        ids, tokens[0], cotangent[0], right, up, diag, bias_a, bias_b, bias_c,
        qkv_one, proj_one, up_one, down_one, merge_weight, qkv_two, proj_two, up_two, down_two,
        select, gather, cot_select, strips, mask, mask_t, fold, *blocks_of_pairs(),
    )
    lon_strip = lax.ppermute(lon_strip, lon, to_right)
    lat_strip = lax.ppermute(lat_strip, "lat", to_up)
    corner = lax.ppermute(corner, both, corner_out)
    other_core = [(i, 1 - i) for i in range(2)]
    theirs_two = lax.ppermute(theirs_two, "core", other_core)
    result = lambda *dims: jax.ShapeDtypeStruct(dims, F32)
    blocks = lambda rows: jax.ShapeDtypeStruct((CHIPS, rows, LANES), BF16)
    chips = ("lat", "chip")
    to_tokens, to_two, place, place_two = output_constants()
    kept = lower_forward(xw, bias_a, bias_b, qkv_one, proj_one, up_one, mask, mask_t, fold)
    normed, full, scale, *others = kept
    *gradients, mine_one, theirs_one = lower(
        ids, grad_own, lon_strip, lat_strip, corner, normed, *others,
        proj_one, up_one, down_one, back_own, back_strips, mask, mask_t, fold,
    )
    theirs_one = lax.ppermute(theirs_one, "core", other_core)
    packed = call(
        chip_kernel, "chip", 3, 24, blocks(UPPER_BLOCK + LOWER_BLOCK),
        (ids, mine_two, theirs_two, mine_one, theirs_one),
    )
    packed = lax.all_to_all(packed, chips, 0, 0, tiled=True)
    strip = lambda count: jax.ShapeDtypeStruct((count, C2), BF16)
    own_cells, own_two, lon_strip, lat_strip, corner = call(
        finish_kernel, "finish", 4, 12,
        (result(288, C2), result(144, C2), *(strip(count) for count in SHIFT)),
        (ids, *gradients, full, scale, out_two, qkv_one, to_tokens, to_two),
        [pltpu.VMEM((576, C1), F32)],
    )
    packed, own_cells = lax.optimization_barrier((packed, own_cells))
    lon_strip = lax.ppermute(lon_strip, lon, to_right)
    lat_strip = lax.ppermute(lat_strip, "lat", to_up)
    corner = lax.ppermute(corner, both, corner_out)
    summed = call(total_kernel, "total", 2, 16, blocks(UPPER_BLOCK + LOWER_BLOCK), (ids, packed))
    gathered = lax.all_to_all(summed, chips, 0, 0, tiled=True)
    weights = (qkv_one, proj_one, up_one, down_one, merge_weight, qkv_two, proj_two, up_two, down_two)
    sums = call(
        functools.partial(last_kernel, factor), "last", 6, 40, tuple(result(*w.shape) for w in weights),
        (ids, gathered, lax.ppermute(gathered, "core", other_core)),
        [
            pltpu.VMEM((2, CHIPS * LOWER_BLOCK, LANES), BF16),
            pltpu.VMEM((2, CHIPS * UPPER_BLOCK, LANES), BF16),
        ],
    )
    own_cells, *sums = lax.optimization_barrier((own_cells, *sums))
    grad_tokens, out_two = call(
        assemble_kernel, "assemble", 3, 8, (result(12, 24, 2 * C1), result(72, 1, 2 * C2)),
        (ids, own_cells, own_two, lon_strip, lat_strip, corner, place, place_two),
    )
    return (out_two.reshape(1, 6, 12, 2 * C2), grad_tokens[None], *sums[:3], sums[3].T, *sums[4:])


def solution(mesh):
    lats, lons = mesh.devices.shape
    mesh = Mesh(mesh.devices.reshape(lats, lons // 2, 2), ("lat", "chip", "core"))
    sharded, copied = P(None, "lat", ("chip", "core"), None), P()
    return jax.shard_map(
        per_device,
        mesh=mesh,
        in_specs=(sharded, sharded) + (copied,) * 11,
        out_specs=(sharded, sharded) + (copied,) * 9,
        check_vma=False,
    )
```
